256 devices in a mesh: seq: 64 (over y_hi, x, z), dp: 4 (over y_lo, core).
Axes of the slice: x: 4, y: 4 (y_hi: 2, y_lo: 2; y = y_hi * 2 + y_lo), z: 8, core: 2. Of those that a mesh axis runs over, the one named last changes fastest.
Arguments:
- signal: bfloat16 [4, 32768, 256], P('dp', 'seq'), may hold values from -6 to 6
- cotangent: bfloat16 [4, 32768, 256], P('dp', 'seq'), may hold values from -6 to 6
- filter_codes: bfloat16 [32768, 256], P('seq'), may hold values from -0.03125 to 0.03125
- keep_mask: int32 [32768, 256], P('seq'), may hold values 0 or 1
- exponents: int32 [256], replicated, may hold values from -2 to 2
- skip: float32 [256], replicated, may hold values from -1 to 1
Outputs:
- input_grad: bfloat16 [4, 32768, 256], P('dp', 'seq')
- filter_grad: float32 [32768, 256], P('seq')
The draws below stay inside these ranges and needn't reach their ends.
All inputs are finite; a program needn't handle non-finite values. No bound on the sum of `keep_mask` on one device may be relied on, other than what follows from the above.
Results may differ from the reference program's by a relative error of at most 0.014.
Values may be sent and summed in bfloat16 or wider, within the bound.
A program may use at most 64 MiB of HBM per device.

```python
import math
import jax
import jax.numpy as jnp

C = 256
L = 32768
SEQS = 4


def with_ends(array, key, least, largest):
    longest = array.shape.index(max(array.shape))
    spots = []
    for shift in (0, 1):
        where = [jax.random.randint(jax.random.fold_in(key, axis), (), 0, length) for axis, length in enumerate(array.shape)]
        where[longest] = (where[longest] + shift) % array.shape[longest]
        spots.append(tuple(where))
    return array.at[spots[0]].set(least).at[spots[1]].set(largest)


def steps_of(key, shape, shards, least, high):
    factor_of = 1.0
    for position, parts in shards:
        draws = jax.random.uniform(jax.random.fold_in(jax.random.fold_in(key, 6), position), (parts,), jnp.float32, least / len(shards), high / len(shards))
        factor_of = factor_of * jnp.repeat(jnp.exp(draws), shape[position] // parts).reshape((-1,) + (1,) * (len(shape) - 1 - position))
    return factor_of


def centred(own_key, shape, deviation, bound, shards=(), held_as=jnp.bfloat16):
    result = deviation * jax.random.normal(own_key, shape, jnp.float32)
    if shards:
        result = result * steps_of(own_key, shape, shards, -0.22, 0.18)
    return jnp.clip(result, -bound, bound).astype(held_as)


def setup_inputs(seed: int = 0) -> dict:
    arg_keys = jax.random.split(jax.random.key(seed), 7)
    return {
        "signal": centred(arg_keys[0], (SEQS, L, C), 1.0, 6.0, ((0, 4), (1, 64))),
        "cotangent": centred(arg_keys[1], (SEQS, L, C), 1.0, 6.0, ((0, 4), (1, 64))),
        "filter_codes": centred(arg_keys[2], (L, C), L ** -0.5, 0.03125, ((0, 64),)),
        "keep_mask": with_ends((jax.random.randint(arg_keys[3], (L, C), 0, 4) < 3).astype(jnp.int32), jax.random.fold_in(arg_keys[3], 1), 0, 1),
        "exponents": with_ends(jax.random.randint(arg_keys[4], (C,), -2, 3), jax.random.fold_in(arg_keys[4], 1), -2, 2).astype(jnp.int32),
        "skip": jnp.clip(jax.random.uniform(arg_keys[5], (C,), jnp.float32, -1.0, 1.0), -1.0, 1.0),
    }


def reference(signal, cotangent, filter_codes, keep_mask, exponents, skip):
    length = signal.shape[1]
    points = 2 * length
    scale = jnp.exp2(exponents.astype(jnp.float32))
    filter_spec = jnp.fft.rfft(filter_codes.astype(jnp.float32), n=points, axis=0)
    grads = []
    total = jnp.zeros((length, signal.shape[2]), jnp.float32)
    for index in range(SEQS):
        back = cotangent[index].astype(jnp.float32)
        back_spec = jnp.fft.rfft(back, n=points, axis=0)
        sig_spec = jnp.fft.rfft(signal[index].astype(jnp.float32), n=points, axis=0)
        conv_back = jnp.fft.irfft(jnp.conj(filter_spec) * back_spec, n=points, axis=0)[:length]
        grads.append((conv_back * scale + skip * back).astype(jnp.bfloat16))
        total = total + jnp.fft.irfft(jnp.conj(sig_spec) * back_spec, n=points, axis=0)[:length]
    input_grad = jnp.stack(grads, axis=0)
    filter_grad = keep_mask.astype(jnp.float32) * scale * total / math.sqrt(SEQS * length)
    return (input_grad, filter_grad)
```

```python
import functools
import math

import jax
import jax.numpy as jnp
import numpy as np
from jax import lax
from jax.experimental import pallas as pl
from jax.experimental.pallas import tpu as pltpu
from jax.sharding import PartitionSpec as P

MESH = pl.DeviceIdType.MESH
F32 = jnp.float32
BF16 = jnp.bfloat16
LANES = 128
ROWS = 4
SEQ = 64
DP = 4
ALL = SEQ * DP
HALF = SEQ * ROWS
POINTS = 2 * HALF * LANES
VMEM_LIMIT = 48 << 20


def split(values):
    high = values.astype(BF16)
    return high, (values - high.astype(F32)).astype(BF16)


def np_split(values):
    values = values.astype(np.float32)
    high = values.astype(jnp.bfloat16)
    return high, (values - high.astype(np.float32)).astype(jnp.bfloat16)


def tables():
    rows = (ROWS * np.arange(SEQ)[None, :] + np.arange(ROWS)[:, None]).reshape(-1)
    odd = 2 * np.arange(HALF) + 1
    angle = 2 * np.pi / (4 * HALF) * ((odd[:, None] * rows[None, :]) % (4 * HALF))
    first = np.concatenate([np.cos(angle), -np.sin(angle)], axis=0)
    lane = np.arange(LANES)
    angle = 2 * np.pi / (2 * POINTS) * ((odd[:, None] * lane[None, :]) % (2 * POINTS))
    turn = np.concatenate([np.cos(angle), -np.sin(angle)], axis=1).astype(np.float32)
    angle = 2 * np.pi / LANES * ((lane[:, None] * lane[None, :]) % LANES)
    cos, sin = np.cos(angle), np.sin(angle)
    second = np.block([[cos, -sin], [sin, cos]])
    first_high, first_low = np_split(first)
    second_high, second_low = np_split(second)
    return (
        np.concatenate([first_high, first_low], axis=1),
        turn,
        np.concatenate([second_high, second_high, second_low], axis=0),
        np.concatenate([second_high.T, second_high.T, second_low.T], axis=0),
        np.concatenate([first_high.T, first_low.T, first_high.T], axis=1),
    )


def dot(left, right):
    return jnp.dot(left, right, preferred_element_type=F32)


def dot_nt(left, right):
    return lax.dot_general(left, right, (((1,), (1,)), ((), ())), preferred_element_type=F32)


def same(shape, offset=0, factor=1):
    row = lax.broadcasted_iota(jnp.int32, shape, 0)
    column = lax.broadcasted_iota(jnp.int32, shape, 1)
    return jnp.where(column == factor * row + offset, 1.0, 0.0).astype(BF16)


def mix(values, matrix):
    high, low = split(values)
    return dot(jnp.concatenate([high, low, high], axis=1), matrix)


def forward(rows, first, turn, second):
    both = dot(first, jnp.concatenate([rows, rows], axis=0))
    real, imag = both[:HALF], both[HALF:]
    cos, sin = turn[:, :LANES], turn[:, LANES:]
    turned = jnp.concatenate([real * cos - imag * sin, real * sin + imag * cos], axis=1)
    return mix(turned, second)


def backward(spectrum, turn, second_back, first_back):
    both = mix(spectrum, second_back)
    real, imag = both[:, :LANES], both[:, LANES:]
    cos, sin = turn[:, :LANES], turn[:, LANES:]
    turned = jnp.concatenate([real * cos + imag * sin, imag * cos - real * sin], axis=0)
    high, low = split(turned)
    return dot(first_back, jnp.concatenate([high, high, low], axis=0))


def conj_product(left, right):
    left_real, left_imag = left[:, :LANES], left[:, LANES:]
    right_real, right_imag = right[:, :LANES], right[:, LANES:]
    return jnp.concatenate(
        [
            left_real * right_real + left_imag * right_imag,
            left_real * right_imag - left_imag * right_real,
        ],
        axis=1,
    )


def main_kernel(
    signal, cotangent, codes, exponents, skip, first, turn, second, second_back, first_back,
    home,
    wide, wide_codes, out_buf, codes_buf, in_buf, codes_in, back_buf, spec_g, spec_h,
    send_sem, recv_sem,
):
    s, d = lax.axis_index("seq"), lax.axis_index("dp")
    me = s * DP + d
    place = d * SEQ + s

    barrier = pltpu.get_barrier_semaphore()

    def greet(step, carry):
        other = lax.rem(me + step, ALL)
        pl.semaphore_signal(
            barrier, inc=1, device_id=(other // DP, lax.rem(other, DP)), device_id_type=MESH
        )
        return carry

    lax.fori_loop(1, ALL, greet, 0, unroll=15)

    eye = same((ALL, ALL))
    for base, array in ((0, signal), (ROWS, cotangent)):
        turned = dot_nt(eye, array[...])
        for row in range(ROWS):
            wide[pl.ds(base + row, ALL, 2 * ROWS), :] = turned[:, row * LANES : (row + 1) * LANES]
    out_buf[...] = wide[...].reshape(ALL, 2 * ROWS, LANES).astype(BF16)
    turned = dot_nt(same((SEQ, ALL), d, DP), codes[...])
    wide_codes[...] = jnp.zeros_like(wide_codes)
    for row in range(ROWS):
        wide_codes[pl.ds(row, SEQ, 2 * ROWS), :] = turned[:, row * LANES : (row + 1) * LANES]
    codes_buf[...] = wide_codes[...].reshape(SEQ, 2 * ROWS, LANES).astype(BF16)

    pl.semaphore_wait(barrier, ALL - 1)

    def send_codes(step, carry):
        other = lax.rem(s + step, SEQ)
        pltpu.make_async_remote_copy(
            src_ref=codes_buf.at[other], dst_ref=codes_in.at[s],
            send_sem=send_sem.at[0], recv_sem=recv_sem.at[0],
            device_id=(other, d), device_id_type=MESH,
        ).start()
        return carry

    lax.fori_loop(1, SEQ, send_codes, 0, unroll=9)

    def send_rows(step, carry):
        other = lax.rem(me + step, ALL)
        pltpu.make_async_remote_copy(
            src_ref=out_buf.at[other], dst_ref=in_buf.at[place],
            send_sem=send_sem.at[1], recv_sem=recv_sem.at[1],
            device_id=(other // DP, lax.rem(other, DP)), device_id_type=MESH,
        ).start()
        return carry

    lax.fori_loop(1, ALL, send_rows, 0, unroll=15)
    codes_in[pl.ds(s, 1)] = codes_buf[pl.ds(s, 1)]
    in_buf[pl.ds(place, 1)] = out_buf[pl.ds(me, 1)]

    def drain(source, target, index, count):
        every = pltpu.make_async_remote_copy(
            src_ref=source.at[pl.ds(0, count)], dst_ref=target.at[pl.ds(0, count)],
            send_sem=send_sem.at[index], recv_sem=recv_sem.at[index],
            device_id=(s, d), device_id_type=MESH,
        )
        every.wait_recv()
        every.wait_send()

    drain(codes_buf, codes_in, 0, SEQ - 1)
    wide_codes[...] = codes_in[...].reshape(SEQ * 2 * ROWS, LANES).astype(F32)
    rows = jnp.concatenate(
        [wide_codes[pl.ds(row, SEQ, 2 * ROWS), :] for row in range(ROWS)], axis=0
    ).astype(BF16)
    spec_h[...] = forward(rows, first[...], turn[...], second[...])

    drain(out_buf, in_buf, 1, ALL - 1)
    wide[...] = in_buf[...].reshape(ALL * 2 * ROWS, LANES).astype(F32)

    unit = jnp.full((1, LANES), exponents[me].astype(F32), F32)
    scale = jnp.exp2(unit) * (2.0 / POINTS)
    direct = skip[me]

    def rows_of(index, base):
        start = index * (SEQ * 2 * ROWS) + base
        return jnp.concatenate(
            [wide[pl.ds(start + row, SEQ, 2 * ROWS), :] for row in range(ROWS)], axis=0
        )

    spec_g[...] = jnp.zeros_like(spec_g)
    for index in range(DP):
        start = index * (SEQ * 2 * ROWS)
        cot = rows_of(index, ROWS)
        cot_spec = forward(cot.astype(BF16), first[...], turn[...], second[...])
        sig_spec = forward(rows_of(index, 0).astype(BF16), first[...], turn[...], second[...])
        spec_g[...] += conj_product(sig_spec, cot_spec)
        back = backward(
            conj_product(spec_h[...], cot_spec), turn[...], second_back[...], first_back[...]
        )
        grad = back * scale + direct * cot
        for row in range(ROWS):
            wide[pl.ds(start + row, SEQ, 2 * ROWS), :] = grad[row * SEQ : (row + 1) * SEQ]
    total = backward(spec_g[...], turn[...], second_back[...], first_back[...]) * (2.0 / POINTS)
    for index in range(DP):
        start = index * (SEQ * 2 * ROWS) + ROWS
        for row in range(ROWS):
            wide[pl.ds(start + row, SEQ, 2 * ROWS), :] = total[row * SEQ : (row + 1) * SEQ]
    back_buf[...] = wide[...].reshape(ALL, 2 * ROWS, LANES).astype(BF16)

    def send_back(step, carry):
        other = lax.rem(me + step, ALL)
        to_seq, to_dp = other // DP, lax.rem(other, DP)
        pltpu.make_async_remote_copy(
            src_ref=back_buf.at[to_dp * SEQ + to_seq], dst_ref=home.at[me],
            send_sem=send_sem.at[2], recv_sem=recv_sem.at[2],
            device_id=(to_seq, to_dp), device_id_type=MESH,
        ).start()
        return carry

    lax.fori_loop(1, ALL, send_back, 0, unroll=15)
    home[pl.ds(me, 1)] = back_buf[pl.ds(place, 1)]
    drain(back_buf, home, 2, ALL - 1)


def last_kernel(home, mask, exponents, input_grad, filter_grad, wide):
    wide[...] = home[...].reshape(ALL * 2 * ROWS, LANES).astype(F32)
    eye = same((LANES, LANES))
    scale = jnp.exp2(exponents[...].astype(F32)) * (1.0 / math.sqrt(DP * HALF * LANES))
    for row in range(ROWS):
        part = pl.ds(row * LANES, LANES)
        grad = wide[pl.ds(row, ALL, 2 * ROWS), :].astype(BF16)
        input_grad[part, :] = dot_nt(eye, grad).astype(BF16)
        total = wide[pl.ds(ROWS + row, ALL, 2 * ROWS), :].astype(BF16)
        filter_grad[part, :] = mask[part, :].astype(F32) * scale * dot_nt(eye, total)


def per_device(signal, cotangent, filter_codes, keep_mask, exponents, skip):
    span, width = signal.shape[1], signal.shape[2]
    vmem = pl.BlockSpec(memory_space=pltpu.VMEM)
    smem = pl.BlockSpec(memory_space=pltpu.SMEM)
    home = pl.pallas_call(
        main_kernel,
        out_shape=jax.ShapeDtypeStruct((ALL, 2 * ROWS, LANES), BF16),
        in_specs=[vmem] * 3 + [smem] * 2 + [vmem] * 5,
        out_specs=vmem,
        scratch_shapes=[
            pltpu.VMEM((ALL * 2 * ROWS, LANES), F32),
            pltpu.VMEM((SEQ * 2 * ROWS, LANES), F32),
            pltpu.VMEM((ALL, 2 * ROWS, LANES), BF16),
            pltpu.VMEM((SEQ, 2 * ROWS, LANES), BF16),
            pltpu.VMEM((ALL, 2 * ROWS, LANES), BF16),
            pltpu.VMEM((SEQ, 2 * ROWS, LANES), BF16),
            pltpu.VMEM((ALL, 2 * ROWS, LANES), BF16),
            pltpu.VMEM((HALF, 2 * LANES), F32),
            pltpu.VMEM((HALF, 2 * LANES), F32),
            pltpu.SemaphoreType.DMA((3,)),
            pltpu.SemaphoreType.DMA((3,)),
        ],
        compiler_params=pltpu.CompilerParams(
            collective_id=0, has_side_effects=True, vmem_limit_bytes=VMEM_LIMIT
        ),
        name="main",
    )(
        signal.reshape(span, width), cotangent.reshape(span, width), filter_codes,
        exponents, skip, *[jnp.asarray(table) for table in tables()],
    )
    input_grad, filter_grad = pl.pallas_call(
        last_kernel,
        out_shape=(
            jax.ShapeDtypeStruct((span, width), BF16),
            jax.ShapeDtypeStruct((span, width), F32),
        ),
        in_specs=[vmem] * 3,
        out_specs=(vmem, vmem),
        scratch_shapes=[pltpu.VMEM((ALL * 2 * ROWS, LANES), F32)],
        compiler_params=pltpu.CompilerParams(vmem_limit_bytes=VMEM_LIMIT),
        name="last",
    )(home, keep_mask, exponents.reshape(1, width))
    return input_grad.reshape(signal.shape), filter_grad


def solution(mesh):
    return jax.shard_map(
        per_device,
        mesh=mesh,
        in_specs=(
            P("dp", "seq", None),
            P("dp", "seq", None),
            P("seq", None),
            P("seq", None),
            P(),
            P(),
        ),
        out_specs=(P("dp", "seq", None), P("seq", None)),
        check_vma=False,
    )
```

```python
import functools
import math

import jax
import jax.numpy as jnp
import numpy as np
from jax import lax
from jax.experimental import pallas as pl
from jax.experimental.pallas import tpu as pltpu
from jax.sharding import PartitionSpec as P

LOGICAL = pl.DeviceIdType.LOGICAL
F32 = jnp.float32
BF16 = jnp.bfloat16
LANES = 128
ROWS = 4
SEQ = 64
DP = 4
ALL = SEQ * DP
HALF = SEQ * ROWS
POINTS = 2 * HALF * LANES
VMEM_LIMIT = 58 << 20


def split(values):
    high = values.astype(BF16)
    return high, (values - high.astype(F32)).astype(BF16)


def np_split(values):
    values = values.astype(np.float32)
    high = values.astype(jnp.bfloat16)
    return high, (values - high.astype(np.float32)).astype(jnp.bfloat16)


def tables():
    rows = (ROWS * np.arange(SEQ)[None, :] + np.arange(ROWS)[:, None]).reshape(-1)
    odd = 2 * np.arange(HALF) + 1
    angle = 2 * np.pi / (4 * HALF) * ((odd[:, None] * rows[None, :]) % (4 * HALF))
    first = np.concatenate([np.cos(angle), -np.sin(angle)], axis=0)
    lane = np.arange(LANES)
    angle = 2 * np.pi / (2 * POINTS) * ((odd[:, None] * lane[None, :]) % (2 * POINTS))
    turn = np.concatenate([np.cos(angle), -np.sin(angle)], axis=1).astype(np.float32)
    angle = 2 * np.pi / LANES * ((lane[:, None] * lane[None, :]) % LANES)
    cos, sin = np.cos(angle), np.sin(angle)
    second = np.block([[cos, -sin], [sin, cos]])
    first_high, first_low = np_split(first)
    second_high, second_low = np_split(second)
    return (
        np.concatenate([first_high, first_low], axis=1),
        turn,
        np.concatenate([second_high, second_high, second_low], axis=0),
        np.concatenate([second_high.T, second_high.T, second_low.T], axis=0),
        np.concatenate([first_high.T, first_low.T, first_high.T], axis=1),
    )


def dot(left, right):
    return jnp.dot(left, right, preferred_element_type=F32)


def dot_nt(left, right):
    return lax.dot_general(left, right, (((1,), (1,)), ((), ())), preferred_element_type=F32)


def same(shape, offset=0, factor=1):
    row = lax.broadcasted_iota(jnp.int32, shape, 0)
    column = lax.broadcasted_iota(jnp.int32, shape, 1)
    return jnp.where(column == factor * row + offset, 1.0, 0.0).astype(BF16)


def mix(values, matrix):
    high, low = split(values)
    return dot(jnp.concatenate([high, low, high], axis=1), matrix)


def forward(rows, first, turn, second):
    both = dot(first, jnp.concatenate([rows, rows], axis=0))
    cos, sin = turn[:, :LANES], turn[:, LANES:]
    spectra = []
    for at in range(0, rows.shape[1], LANES):
        real, imag = both[:HALF, at : at + LANES], both[HALF:, at : at + LANES]
        turned = jnp.concatenate([real * cos - imag * sin, real * sin + imag * cos], axis=1)
        spectra.append(mix(turned, second))
    return spectra


def backward(spectra, turn, second_back, first_back):
    cos, sin = turn[:, :LANES], turn[:, LANES:]
    columns = []
    for spectrum in spectra:
        both = mix(spectrum, second_back)
        real, imag = both[:, :LANES], both[:, LANES:]
        columns.append(
            jnp.concatenate([real * cos + imag * sin, imag * cos - real * sin], axis=0)
        )
    high, low = split(jnp.concatenate(columns, axis=1))
    return dot(first_back, jnp.concatenate([high, high, low], axis=0))


def conj_product(left, right):
    left_real, left_imag = left[:, :LANES], left[:, LANES:]
    right_real, right_imag = right[:, :LANES], right[:, LANES:]
    return jnp.concatenate(
        [
            left_real * right_real + left_imag * right_imag,
            left_real * right_imag - left_imag * right_real,
        ],
        axis=1,
    )


def spread(wide, values, count):
    for row in range(ROWS):
        wide[pl.ds(0, count), row, :] = values[:, row * LANES : (row + 1) * LANES]
    return wide[pl.ds(0, count)].astype(BF16)


def gather(wide, start):
    return jnp.concatenate([wide[pl.ds(start, SEQ), row, :] for row in range(ROWS)], axis=0)


def main_kernel(
    signal_hbm, cotangent_hbm, codes_hbm, exponents, skip,
    first_hbm, turn_hbm, second_hbm, second_back_hbm, first_back_hbm,
    home_grad, home_total,
    signal, cotangent, codes, first, turn, second, second_back, first_back,
    wide, codes_out, cot_out, sig_out, codes_in, cot_in, sig_in, grad_out, total_out,
    cot_spec, send_sem, recv_sem, load_sem,
):
    loads = [
        pltpu.make_async_copy(source, target, load_sem.at[index])
        for index, (source, target) in enumerate(
            (
                (codes_hbm, codes), (cotangent_hbm, cotangent), (signal_hbm, signal),
                (first_hbm, first), (turn_hbm, turn), (second_hbm, second),
                (second_back_hbm, second_back), (first_back_hbm, first_back),
            )
        )
    ]
    for load in loads:
        load.start()
    s, d = lax.axis_index("seq"), lax.axis_index("dp")
    me = s * DP + d
    place = d * SEQ + s
    barrier = pltpu.get_barrier_semaphore()

    def greet(step, carry):
        other = lax.rem(me + step, ALL)
        pl.semaphore_signal(barrier, inc=1, device_id=other, device_id_type=LOGICAL)
        return carry

    lax.fori_loop(1, ALL, greet, 0, unroll=15)

    def post(index, source, target, other):
        pltpu.make_async_remote_copy(
            src_ref=source, dst_ref=target,
            send_sem=send_sem.at[index], recv_sem=recv_sem.at[index],
            device_id=other, device_id_type=LOGICAL,
        ).start()

    def drain(index, array, count):
        part = array.at[pl.ds(0, count)]
        return pltpu.make_async_remote_copy(
            src_ref=part, dst_ref=part,
            send_sem=send_sem.at[index], recv_sem=recv_sem.at[index],
            device_id=me, device_id_type=LOGICAL,
        )

    loads[0].wait()
    codes_out[...] = spread(wide, dot_nt(same((SEQ, ALL), d, DP), codes[...]), SEQ)
    loads[1].wait()
    eye = same((ALL, ALL))
    cot_out[...] = spread(wide, dot_nt(eye, cotangent[...]), ALL)
    pl.semaphore_wait(barrier, ALL - 1)

    def send_codes(step, carry):
        other = lax.rem(s + step, SEQ)
        post(0, codes_out.at[other], codes_in.at[s], other * DP + d)
        return carry

    lax.fori_loop(1, SEQ, send_codes, 0, unroll=9)

    def send_cot(step, carry):
        other = lax.rem(me + step, ALL)
        post(1, cot_out.at[other], cot_in.at[place], other)
        return carry

    lax.fori_loop(1, ALL, send_cot, 0, unroll=15)

    loads[2].wait()
    sig_out[...] = spread(wide, dot_nt(eye, signal[...]), ALL)

    def send_sig(step, carry):
        other = lax.rem(me + step, ALL)
        post(2, sig_out.at[other], sig_in.at[place], other)
        return carry

    lax.fori_loop(1, ALL, send_sig, 0, unroll=15)
    codes_in[pl.ds(s, 1)] = codes_out[pl.ds(s, 1)]
    cot_in[pl.ds(place, 1)] = cot_out[pl.ds(me, 1)]
    sig_in[pl.ds(place, 1)] = sig_out[pl.ds(me, 1)]
    for load in loads[3:]:
        load.wait()
    unit = jnp.full((1, LANES), exponents[me].astype(F32), F32)
    scale = jnp.exp2(unit) * (2.0 / POINTS)
    direct = skip[me]

    drain(0, codes_in, SEQ - 1).wait_recv()
    wide[pl.ds(0, SEQ)] = codes_in[...].astype(F32)
    (codes_spec,) = forward(gather(wide, 0).astype(BF16), first[...], turn[...], second[...])

    drain(1, cot_in, ALL - 1).wait_recv()
    wide[...] = cot_in[...].astype(F32)
    for pair in (0, 2):
        dps = [lax.rem(d + pair + index, DP) for index in range(2)]
        cots = [gather(wide, which * SEQ) for which in dps]
        both = jnp.concatenate(cots, axis=1)
        spectra = forward(both.astype(BF16), first[...], turn[...], second[...])
        for index, spectrum in enumerate(spectra):
            cot_spec[pair + index] = spectrum
        back = backward(
            [conj_product(codes_spec, spectrum) for spectrum in spectra],
            turn[...], second_back[...], first_back[...],
        )
        for index, which in enumerate(dps):
            grad = back[:, index * LANES : (index + 1) * LANES] * scale + direct * cots[index]
            for row in range(ROWS):
                wide[pl.ds(which * SEQ, SEQ), row, :] = grad[row * SEQ : (row + 1) * SEQ]
            grad_out[pl.ds(which * SEQ, SEQ)] = wide[pl.ds(which * SEQ, SEQ)].astype(BF16)

            def send_grad(step, carry, which=which):
                to_seq = lax.rem(s + step, SEQ)
                post(3, grad_out.at[which * SEQ + to_seq], home_grad.at[me], to_seq * DP + which)
                return carry

            if pair + index == 0:
                home_grad[pl.ds(me, 1)] = grad_out[pl.ds(place, 1)]
                lax.fori_loop(1, SEQ, send_grad, 0, unroll=9)
            else:
                lax.fori_loop(0, SEQ, send_grad, 0, unroll=8)

    drain(2, sig_in, ALL - 1).wait_recv()
    wide[...] = sig_in[...].astype(F32)
    total_spec = jnp.zeros((HALF, 2 * LANES), F32)
    for pair in (0, 2):
        dps = [lax.rem(d + pair + index, DP) for index in range(2)]
        both = jnp.concatenate([gather(wide, which * SEQ) for which in dps], axis=1)
        spectra = forward(both.astype(BF16), first[...], turn[...], second[...])
        for index, spectrum in enumerate(spectra):
            total_spec += conj_product(spectrum, cot_spec[pair + index])
    total = backward([total_spec], turn[...], second_back[...], first_back[...])
    total = total * (2.0 / POINTS)
    for row in range(ROWS):
        wide[pl.ds(0, SEQ), row, :] = total[row * SEQ : (row + 1) * SEQ]
    total_out[...] = wide[pl.ds(0, SEQ)].astype(BF16)

    def send_total(step, carry):
        other = lax.rem(me + step, ALL)
        post(4, total_out.at[other // DP], home_total.at[me], other)
        return carry

    lax.fori_loop(1, ALL, send_total, 0, unroll=15)
    home_total[pl.ds(me, 1)] = total_out[pl.ds(s, 1)]
    drain(0, codes_out, SEQ - 1).wait_send()
    drain(1, cot_out, ALL - 1).wait_send()
    drain(2, sig_out, ALL - 1).wait_send()
    drain(3, grad_out, ALL - 1).wait_send()
    drain(4, home_total, ALL - 1).wait_send()
    drain(3, home_grad, ALL - 1).wait_recv()
    drain(4, home_total, ALL - 1).wait_recv()


def last_kernel(home_grad, home_total, mask_hbm, exponents, input_grad, filter_grad, wide, mask, load_sem):
    load = pltpu.make_async_copy(mask_hbm, mask, load_sem)
    load.start()
    eye = same((LANES, LANES))
    wide[...] = home_grad[...].astype(F32)
    for row in range(ROWS):
        part = pl.ds(row * LANES, LANES)
        input_grad[part, :] = dot_nt(eye, wide[:, row, :].astype(BF16)).astype(BF16)
    scale = jnp.exp2(exponents[...].astype(F32)) * (1.0 / math.sqrt(DP * HALF * LANES))
    wide[...] = home_total[...].astype(F32)
    load.wait()
    for row in range(ROWS):
        part = pl.ds(row * LANES, LANES)
        total = dot_nt(eye, wide[:, row, :].astype(BF16))
        filter_grad[part, :] = mask[part, :].astype(F32) * scale * total


def per_device(signal, cotangent, filter_codes, keep_mask, exponents, skip):
    span, width = signal.shape[1], signal.shape[2]
    vmem = pl.BlockSpec(memory_space=pltpu.VMEM)
    smem = pl.BlockSpec(memory_space=pltpu.SMEM)
    hbm = pl.BlockSpec(memory_space=pltpu.HBM)
    constants = [jnp.asarray(table) for table in tables()]
    message = (ROWS, LANES)
    home_grad, home_total = pl.pallas_call(
        main_kernel,
        out_shape=(jax.ShapeDtypeStruct((ALL,) + message, BF16),) * 2,
        in_specs=[hbm] * 3 + [smem] * 2 + [hbm] * 5,
        out_specs=(vmem, vmem),
        scratch_shapes=[
            pltpu.VMEM((span, width), BF16),
            pltpu.VMEM((span, width), BF16),
            pltpu.VMEM((span, width), BF16),
            *[pltpu.VMEM(table.shape, table.dtype) for table in constants],
            pltpu.VMEM((ALL,) + message, F32),
            pltpu.VMEM((SEQ,) + message, BF16),
            pltpu.VMEM((ALL,) + message, BF16),
            pltpu.VMEM((ALL,) + message, BF16),
            pltpu.VMEM((SEQ,) + message, BF16),
            pltpu.VMEM((ALL,) + message, BF16),
            pltpu.VMEM((ALL,) + message, BF16),
            pltpu.VMEM((ALL,) + message, BF16),
            pltpu.VMEM((SEQ,) + message, BF16),
            pltpu.VMEM((DP, HALF, 2 * LANES), F32),
            pltpu.SemaphoreType.DMA((5,)),
            pltpu.SemaphoreType.DMA((5,)),
            pltpu.SemaphoreType.DMA((8,)),
        ],
        compiler_params=pltpu.CompilerParams(
            collective_id=0, has_side_effects=True, vmem_limit_bytes=VMEM_LIMIT
        ),
        name="main",
    )(
        signal.reshape(span, width), cotangent.reshape(span, width), filter_codes,
        exponents, skip, *constants,
    )
    input_grad, filter_grad = pl.pallas_call(
        last_kernel,
        out_shape=(
            jax.ShapeDtypeStruct((span, width), BF16),
            jax.ShapeDtypeStruct((span, width), F32),
        ),
        in_specs=[vmem, vmem, hbm, vmem],
        out_specs=(vmem, vmem),
        scratch_shapes=[
            pltpu.VMEM((ALL,) + message, F32),
            pltpu.VMEM((span, width), jnp.int32),
            pltpu.SemaphoreType.DMA,
        ],
        compiler_params=pltpu.CompilerParams(vmem_limit_bytes=VMEM_LIMIT),
        name="last",
    )(home_grad, home_total, keep_mask, exponents.reshape(1, width))
    return input_grad.reshape(signal.shape), filter_grad


def solution(mesh):
    return jax.shard_map(
        per_device,
        mesh=mesh,
        in_specs=(
            P("dp", "seq", None),
            P("dp", "seq", None),
            P("seq", None),
            P("seq", None),
            P(),
            P(),
        ),
        out_specs=(P("dp", "seq", None), P("seq", None)),
        check_vma=False,
    )
```

```python
import functools
import math

import jax
import jax.numpy as jnp
import numpy as np
from jax import lax
from jax.experimental import pallas as pl
from jax.experimental.pallas import tpu as pltpu
from jax.sharding import PartitionSpec as P

LOGICAL = pl.DeviceIdType.LOGICAL
F32 = jnp.float32
BF16 = jnp.bfloat16
LANES = 128
ROWS = 4
SEQ = 64
DP = 4
ALL = SEQ * DP
HALF = SEQ * ROWS
POINTS = 2 * HALF * LANES
Z, X, Y = 8, 4, 2
VMEM_LIMIT = 58 << 20


def split(values):
    high = values.astype(BF16)
    return high, (values - high.astype(F32)).astype(BF16)


def np_split(values):
    values = values.astype(np.float32)
    high = values.astype(jnp.bfloat16)
    return high, (values - high.astype(np.float32)).astype(jnp.bfloat16)


def tables():
    rows = (ROWS * np.arange(SEQ)[None, :] + np.arange(ROWS)[:, None]).reshape(-1)
    odd = 2 * np.arange(HALF) + 1
    angle = 2 * np.pi / (4 * HALF) * ((odd[:, None] * rows[None, :]) % (4 * HALF))
    first = np.concatenate([np.cos(angle), -np.sin(angle)], axis=0)
    lane = np.arange(LANES)
    angle = 2 * np.pi / (2 * POINTS) * ((odd[:, None] * lane[None, :]) % (2 * POINTS))
    turn = np.concatenate([np.cos(angle), -np.sin(angle)], axis=1).astype(np.float32)
    angle = 2 * np.pi / LANES * ((lane[:, None] * lane[None, :]) % LANES)
    cos, sin = np.cos(angle), np.sin(angle)
    second = np.block([[cos, -sin], [sin, cos]])
    first_high, first_low = np_split(first)
    second_high, second_low = np_split(second)
    return (
        np.concatenate([first_high, first_low], axis=1),
        turn,
        np.concatenate([second_high, second_high, second_low], axis=0),
        np.concatenate([second_high.T, second_high.T, second_low.T], axis=0),
        np.concatenate([first_high.T, first_low.T, first_high.T], axis=1),
    )


def dot(left, right):
    return jnp.dot(left, right, preferred_element_type=F32)


def dot_nt(left, right):
    return lax.dot_general(left, right, (((1,), (1,)), ((), ())), preferred_element_type=F32)


def same(shape, offset=0, factor=1):
    row = lax.broadcasted_iota(jnp.int32, shape, 0)
    column = lax.broadcasted_iota(jnp.int32, shape, 1)
    return jnp.where(column == factor * row + offset, 1.0, 0.0).astype(BF16)


def mix(values, matrix):
    high, low = split(values)
    return dot(jnp.concatenate([high, low, high], axis=1), matrix)


def forward(rows, first, turn, second):
    both = dot(first, jnp.concatenate([rows, rows], axis=0))
    cos, sin = turn[:, :LANES], turn[:, LANES:]
    spectra = []
    for at in range(0, rows.shape[1], LANES):
        real, imag = both[:HALF, at : at + LANES], both[HALF:, at : at + LANES]
        turned = jnp.concatenate([real * cos - imag * sin, real * sin + imag * cos], axis=1)
        spectra.append(mix(turned, second))
    return spectra


def backward(spectra, turn, second_back, first_back):
    cos, sin = turn[:, :LANES], turn[:, LANES:]
    columns = []
    for spectrum in spectra:
        both = mix(spectrum, second_back)
        real, imag = both[:, :LANES], both[:, LANES:]
        columns.append(
            jnp.concatenate([real * cos + imag * sin, imag * cos - real * sin], axis=0)
        )
    high, low = split(jnp.concatenate(columns, axis=1))
    return dot(first_back, jnp.concatenate([high, high, low], axis=0))


def conj_product(left, right):
    left_real, left_imag = left[:, :LANES], left[:, LANES:]
    right_real, right_imag = right[:, :LANES], right[:, LANES:]
    return jnp.concatenate(
        [
            left_real * right_real + left_imag * right_imag,
            left_real * right_imag - left_imag * right_real,
        ],
        axis=1,
    )


def hops(near):
    def distance(step):
        up, across, along, side, _ = step
        return min(along, Z - along) + min(across, X - across) + (2 * up + side) % 3 + up * side

    steps = [
        (up, across, along, side, core)
        for along in range(Z)
        for across in range(X)
        for up in range(Y)
        for side, core in near
    ]
    steps.sort(key=lambda step: -distance(step))
    return steps


DP_STEPS = ((0, 0), (0, 1), (1, 0), (1, 1))


def spread(wide, values, count):
    for row in range(ROWS):
        wide[pl.ds(0, count), row, :] = values[:, row * LANES : (row + 1) * LANES]
    return wide[pl.ds(0, count)].astype(BF16)


def gather(wide, start):
    return jnp.concatenate([wide[pl.ds(start, SEQ), row, :] for row in range(ROWS)], axis=0)


def main_kernel(
    signal_hbm, cotangent_hbm, codes_hbm, mask_hbm, exponents, skip, powers_hbm,
    first_hbm, turn_hbm, second_hbm, second_back_hbm, first_back_hbm,
    input_hbm, filter_hbm,
    signal, cotangent, codes, mask, powers, first, turn, second, second_back, first_back,
    wide, codes_out, cot_out, sig_out, codes_in, cot_in, sig_in, grad_out, total_out,
    home_grad, home_total, input_grad, filter_grad,
    cot_spec, send_sem, recv_sem, load_sem, store_sem,
):
    loads = [
        pltpu.make_async_copy(source, target, load_sem.at[index])
        for index, (source, target) in enumerate(
            (
                (codes_hbm, codes), (cotangent_hbm, cotangent), (signal_hbm, signal),
                (first_hbm, first), (turn_hbm, turn), (second_hbm, second),
                (second_back_hbm, second_back), (first_back_hbm, first_back),
                (powers_hbm, powers), (mask_hbm, mask),
            )
        )
    ]
    for load in loads:
        load.start()
    s, d = lax.axis_index("seq"), lax.axis_index("dp")
    me = s * DP + d
    side, core = d // 2, lax.rem(d, 2)
    q = core * 2 + side
    place = q * SEQ + s
    along = [lax.rem(s + step, Z) for step in range(Z)]
    across = [lax.rem(s // Z + step, X) * Z for step in range(X)]
    up = [lax.rem(s // (Z * X) + step, Y) * (Z * X) for step in range(Y)]
    sides = [lax.rem(side + step, 2) for step in range(2)]
    cores = [lax.rem(core + step, 2) for step in range(2)]

    def target(step):
        to_seq = up[step[0]] + across[step[1]] + along[step[2]]
        to_side, to_core = sides[step[3]], cores[step[4]]
        return to_seq, to_core * 2 + to_side, to_seq * DP + to_side * 2 + to_core

    everyone = [step for step in hops(DP_STEPS) if any(step)]
    barrier = pltpu.get_barrier_semaphore()
    for step in everyone:
        pl.semaphore_signal(barrier, inc=1, device_id=target(step)[2], device_id_type=LOGICAL)

    def post(index, source, destination, other):
        pltpu.make_async_remote_copy(
            src_ref=source, dst_ref=destination,
            send_sem=send_sem.at[index], recv_sem=recv_sem.at[index],
            device_id=other, device_id_type=LOGICAL,
        ).start()

    def drain(index, array, count):
        part = array.at[pl.ds(0, count)]
        return pltpu.make_async_remote_copy(
            src_ref=part, dst_ref=part,
            send_sem=send_sem.at[index], recv_sem=recv_sem.at[index],
            device_id=me, device_id_type=LOGICAL,
        )

    loads[0].wait()
    codes_out[...] = spread(wide, dot_nt(same((SEQ, ALL), q * SEQ), codes[...]), SEQ)
    loads[1].wait()
    eye = same((ALL, ALL))
    cot_out[...] = spread(wide, dot_nt(eye, cotangent[...]), ALL)
    pl.semaphore_wait(barrier, ALL - 1)

    for step in hops(((0, 0),)):
        if any(step):
            to_seq, _, other = target(step)
            post(0, codes_out.at[to_seq], codes_in.at[s], other)
    for step in everyone:
        to_seq, to_q, other = target(step)
        post(1, cot_out.at[to_q * SEQ + to_seq], cot_in.at[place], other)

    loads[2].wait()
    sig_out[...] = spread(wide, dot_nt(eye, signal[...]), ALL)
    for step in everyone:
        to_seq, to_q, other = target(step)
        post(2, sig_out.at[to_q * SEQ + to_seq], sig_in.at[place], other)
    codes_in[pl.ds(s, 1)] = codes_out[pl.ds(s, 1)]
    cot_in[pl.ds(place, 1)] = cot_out[pl.ds(place, 1)]
    sig_in[pl.ds(place, 1)] = sig_out[pl.ds(place, 1)]
    for load in loads[3:]:
        load.wait()
    unit = jnp.full((1, LANES), exponents[place].astype(F32), F32)
    scale = jnp.exp2(unit) * (2.0 / POINTS)
    direct = skip[place]

    drain(0, codes_in, SEQ - 1).wait_recv()
    wide[pl.ds(0, SEQ)] = codes_in[...].astype(F32)
    (codes_spec,) = forward(gather(wide, 0).astype(BF16), first[...], turn[...], second[...])

    drain(1, cot_in, ALL - 1).wait_recv()
    wide[...] = cot_in[...].astype(F32)
    for pair in (0, 2):
        near = DP_STEPS[pair : pair + 2]
        which = [cores[step[1]] * 2 + sides[step[0]] for step in near]
        cots = [gather(wide, index * SEQ) for index in which]
        both = jnp.concatenate(cots, axis=1)
        spectra = forward(both.astype(BF16), first[...], turn[...], second[...])
        for index, spectrum in enumerate(spectra):
            cot_spec[pair + index] = spectrum
        back = backward(
            [conj_product(codes_spec, spectrum) for spectrum in spectra],
            turn[...], second_back[...], first_back[...],
        )
        for index in range(2):
            grad = back[:, index * LANES : (index + 1) * LANES] * scale + direct * cots[index]
            part = pl.ds(which[index] * SEQ, SEQ)
            for row in range(ROWS):
                wide[part, row, :] = grad[row * SEQ : (row + 1) * SEQ]
            grad_out[part] = wide[part].astype(BF16)
            for step in hops((near[index],)):
                if any(step):
                    to_seq, to_q, other = target(step)
                    post(3, grad_out.at[to_q * SEQ + to_seq], home_grad.at[place], other)

    drain(2, sig_in, ALL - 1).wait_recv()
    wide[...] = sig_in[...].astype(F32)
    total_spec = jnp.zeros((HALF, 2 * LANES), F32)
    for pair in (0, 2):
        near = DP_STEPS[pair : pair + 2]
        which = [cores[step[1]] * 2 + sides[step[0]] for step in near]
        both = jnp.concatenate([gather(wide, index * SEQ) for index in which], axis=1)
        spectra = forward(both.astype(BF16), first[...], turn[...], second[...])
        for index, spectrum in enumerate(spectra):
            total_spec += conj_product(spectrum, cot_spec[pair + index])
    total = backward([total_spec], turn[...], second_back[...], first_back[...])
    total = total * (2.0 / POINTS)
    for row in range(ROWS):
        wide[pl.ds(0, SEQ), row, :] = total[row * SEQ : (row + 1) * SEQ]
    total_out[...] = wide[pl.ds(0, SEQ)].astype(BF16)
    for step in hops(((0, 0), (1, 0))):
        if any(step):
            to_seq, _, other = target(step)
            post(4, total_out.at[to_seq], home_total.at[place], other)
    home_total[pl.ds(place, 1)] = total_out[pl.ds(s, 1)]
    home_grad[pl.ds(place, 1)] = grad_out[pl.ds(place, 1)]

    eye = same((LANES, LANES))
    drain(3, home_grad, ALL - 1).wait_recv()
    wide[...] = home_grad[...].astype(F32)
    for row in range(ROWS):
        grad = wide[:, row, :].astype(BF16)
        input_grad[pl.ds(row * LANES, LANES), :] = dot_nt(eye, grad).astype(BF16)
    store_input = pltpu.make_async_copy(input_grad, input_hbm, store_sem.at[0])
    store_input.start()

    half = 2 * SEQ
    drain(4, home_total, half - 1).wait_recv()
    mine = home_total.at[pl.ds(core * half, half)]
    across_core = pltpu.make_async_remote_copy(
        src_ref=mine, dst_ref=mine, send_sem=send_sem.at[5], recv_sem=recv_sem.at[5],
        device_id=me + 1 - 2 * core, device_id_type=LOGICAL,
    )
    across_core.start()
    factor = jnp.exp2(powers[...].astype(F32)) * (1.0 / math.sqrt(DP * HALF * LANES))

    def finish(which):
        channels = pl.ds(pl.multiple_of(which * half, LANES), half)
        wide[pl.ds(0, half)] = home_total[pl.ds(which * half, half)].astype(F32)
        chosen = jnp.where(which == 0, factor[:, :half], factor[:, half:])
        for row in range(ROWS):
            part = pl.ds(row * LANES, LANES)
            value = dot_nt(eye, wide[pl.ds(0, half), row, :].astype(BF16))
            filter_grad[part, channels] = mask[part, channels].astype(F32) * chosen * value

    finish(core)
    across_core.wait_recv()
    finish(1 - core)
    store_filter = pltpu.make_async_copy(filter_grad, filter_hbm, store_sem.at[1])
    store_filter.start()
    drain(0, codes_out, SEQ - 1).wait_send()
    drain(1, cot_out, ALL - 1).wait_send()
    drain(2, sig_out, ALL - 1).wait_send()
    drain(3, grad_out, ALL - 1).wait_send()
    drain(4, home_total, half - 1).wait_send()
    across_core.wait_send()
    store_input.wait()
    store_filter.wait()


def last_kernel(input_main, filter_main, input_grad, filter_grad, input_held, filter_held, sem):
    steps = []
    for source, held, result in (
        (filter_main, filter_held, filter_grad), (input_main, input_held, input_grad)
    ):
        size = source.shape[0] // 4
        for index in range(4):
            part = pl.ds(index * size, size)
            at = len(steps)
            steps.append(
                (
                    pltpu.make_async_copy(source.at[part], held.at[part], sem.at[0, at]),
                    pltpu.make_async_copy(held.at[part], result.at[part], sem.at[1, at]),
                )
            )
    for load, _ in steps:
        load.start()
    for load, store in steps:
        load.wait()
        store.start()
    for _, store in steps:
        store.wait()


def per_device(signal, cotangent, filter_codes, keep_mask, exponents, skip):
    span, width = signal.shape[1], signal.shape[2]
    smem = pl.BlockSpec(memory_space=pltpu.SMEM)
    hbm = pl.BlockSpec(memory_space=pltpu.HBM)
    constants = [jnp.asarray(table) for table in tables()]
    message = (ROWS, LANES)
    results = (
        jax.ShapeDtypeStruct((span, width), BF16),
        jax.ShapeDtypeStruct((span, width), F32),
    )
    input_main, filter_main = pl.pallas_call(
        main_kernel,
        out_shape=results,
        in_specs=[hbm] * 4 + [smem] * 2 + [hbm] * 6,
        out_specs=(hbm, hbm),
        scratch_shapes=[
            pltpu.VMEM((span, width), BF16),
            pltpu.VMEM((span, width), BF16),
            pltpu.VMEM((span, width), BF16),
            pltpu.VMEM((span, width), jnp.int32),
            pltpu.VMEM((1, width), jnp.int32),
            *[pltpu.VMEM(table.shape, table.dtype) for table in constants],
            pltpu.VMEM((ALL,) + message, F32),
            pltpu.VMEM((SEQ,) + message, BF16),
            pltpu.VMEM((ALL,) + message, BF16),
            pltpu.VMEM((ALL,) + message, BF16),
            pltpu.VMEM((SEQ,) + message, BF16),
            pltpu.VMEM((ALL,) + message, BF16),
            pltpu.VMEM((ALL,) + message, BF16),
            pltpu.VMEM((ALL,) + message, BF16),
            pltpu.VMEM((SEQ,) + message, BF16),
            pltpu.VMEM((ALL,) + message, BF16),
            pltpu.VMEM((ALL,) + message, BF16),
            pltpu.VMEM((span, width), BF16),
            pltpu.VMEM((span, width), F32),
            pltpu.VMEM((DP, HALF, 2 * LANES), F32),
            pltpu.SemaphoreType.DMA((6,)),
            pltpu.SemaphoreType.DMA((6,)),
            pltpu.SemaphoreType.DMA((10,)),
            pltpu.SemaphoreType.DMA((2,)),
        ],
        compiler_params=pltpu.CompilerParams(
            collective_id=0, has_side_effects=True, vmem_limit_bytes=VMEM_LIMIT
        ),
        name="main",
    )(
        signal.reshape(span, width), cotangent.reshape(span, width), filter_codes, keep_mask,
        exponents, skip, exponents.reshape(1, width), *constants,
    )
    input_grad, filter_grad = pl.pallas_call(
        last_kernel,
        out_shape=results,
        in_specs=[hbm, hbm],
        out_specs=(hbm, hbm),
        scratch_shapes=[
            pltpu.VMEM((span, width), BF16),
            pltpu.VMEM((span, width), F32),
            pltpu.SemaphoreType.DMA((2, 8)),
        ],
        compiler_params=pltpu.CompilerParams(vmem_limit_bytes=VMEM_LIMIT),
        name="last",
    )(input_main, filter_main)
    return input_grad.reshape(signal.shape), filter_grad


def solution(mesh):
    return jax.shard_map(
        per_device,
        mesh=mesh,
        in_specs=(
            P("dp", "seq", None),
            P("dp", "seq", None),
            P("seq", None),
            P("seq", None),
            P(),
            P(),
        ),
        out_specs=(P("dp", "seq", None), P("seq", None)),
        check_vma=False,
    )
```

```python
import functools
import math

import jax
import jax.numpy as jnp
import numpy as np
from jax import lax
from jax.experimental import pallas as pl
from jax.experimental.pallas import tpu as pltpu
from jax.sharding import PartitionSpec as P

LOGICAL = pl.DeviceIdType.LOGICAL
F32 = jnp.float32
BF16 = jnp.bfloat16
LANES = 128
ROWS = 4
SEQ = 64
DP = 4
ALL = SEQ * DP
HALF = SEQ * ROWS
POINTS = 2 * HALF * LANES
Z, X, Y = 8, 4, 2
VMEM_LIMIT = 58 << 20


def split(values):
    high = values.astype(BF16)
    return high, (values - high.astype(F32)).astype(BF16)


def np_split(values):
    values = values.astype(np.float32)
    high = values.astype(jnp.bfloat16)
    return high, (values - high.astype(np.float32)).astype(jnp.bfloat16)


def tables():
    rows = (ROWS * np.arange(SEQ)[None, :] + np.arange(ROWS)[:, None]).reshape(-1)
    odd = 2 * np.arange(HALF) + 1
    angle = 2 * np.pi / (4 * HALF) * ((odd[:, None] * rows[None, :]) % (4 * HALF))
    first = np.concatenate([np.cos(angle), -np.sin(angle)], axis=0)
    lane = np.arange(LANES)
    angle = 2 * np.pi / (2 * POINTS) * ((odd[:, None] * lane[None, :]) % (2 * POINTS))
    turn = np.concatenate([np.cos(angle), -np.sin(angle)], axis=1).astype(np.float32)
    angle = 2 * np.pi / LANES * ((lane[:, None] * lane[None, :]) % LANES)
    cos, sin = np.cos(angle), np.sin(angle)
    second = np.block([[cos, -sin], [sin, cos]])
    first_high, first_low = np_split(first)
    second_high, second_low = np_split(second)
    return (
        np.concatenate([first_high, first_low], axis=1),
        turn,
        np.concatenate([second_high, second_high, second_low], axis=0),
        np.concatenate([second_high.T, second_high.T, second_low.T], axis=0),
        np.concatenate([first_high.T, first_low.T, first_high.T], axis=1),
    )


def dot(left, right):
    return jnp.dot(left, right, preferred_element_type=F32)


def dot_nt(left, right):
    return lax.dot_general(left, right, (((1,), (1,)), ((), ())), preferred_element_type=F32)


def same(shape, offset=0, factor=1):
    row = lax.broadcasted_iota(jnp.int32, shape, 0)
    column = lax.broadcasted_iota(jnp.int32, shape, 1)
    return jnp.where(column == factor * row + offset, 1.0, 0.0).astype(BF16)


def mix(values, matrix):
    high, low = split(values)
    return dot(jnp.concatenate([high, low, high], axis=1), matrix)


def forward(rows, first, turn, second):
    both = dot(first, jnp.concatenate([rows, rows], axis=0))
    cos, sin = turn[:, :LANES], turn[:, LANES:]
    spectra = []
    for at in range(0, rows.shape[1], LANES):
        real, imag = both[:HALF, at : at + LANES], both[HALF:, at : at + LANES]
        turned = jnp.concatenate([real * cos - imag * sin, real * sin + imag * cos], axis=1)
        spectra.append(mix(turned, second))
    return spectra


def backward(spectra, turn, second_back, first_back):
    cos, sin = turn[:, :LANES], turn[:, LANES:]
    columns = []
    for spectrum in spectra:
        both = mix(spectrum, second_back)
        real, imag = both[:, :LANES], both[:, LANES:]
        columns.append(
            jnp.concatenate([real * cos + imag * sin, imag * cos - real * sin], axis=0)
        )
    high, low = split(jnp.concatenate(columns, axis=1))
    return dot(first_back, jnp.concatenate([high, high, low], axis=0))


def conj_product(left, right):
    left_real, left_imag = left[:, :LANES], left[:, LANES:]
    right_real, right_imag = right[:, :LANES], right[:, LANES:]
    return jnp.concatenate(
        [
            left_real * right_real + left_imag * right_imag,
            left_real * right_imag - left_imag * right_real,
        ],
        axis=1,
    )


EARLY = 191
DP_STEPS = ((1, 1), (1, 0), (0, 1), (0, 0))


def hops(near):
    def distance(step):
        up, across, along, side, _ = step
        turns = min(across, X - across) + ((0, 1), (2, 1))[up][side]
        return 2 * turns + min(along, Z - along)

    steps = [
        (up, across, along, side, core)
        for along in range(Z)
        for across in range(X)
        for up in range(Y)
        for side, core in near
    ]
    steps.sort(key=lambda step: -distance(step))
    return steps


def spread(wide, values, count):
    for row in range(ROWS):
        wide[pl.ds(0, count), row, :] = values[:, row * LANES : (row + 1) * LANES]
    return wide[pl.ds(0, count)].astype(BF16)


def gather(wide, start):
    return jnp.concatenate([wide[pl.ds(start, SEQ), row, :] for row in range(ROWS)], axis=0)


def main_kernel(
    signal_hbm, cotangent_hbm, codes_hbm, mask_hbm, exponents, skip, powers_hbm,
    first_hbm, turn_hbm, second_hbm, second_back_hbm, first_back_hbm,
    input_hbm, filter_hbm,
    signal, cotangent, codes, mask, powers, first, turn, second, second_back, first_back,
    wide, codes_out, cot_out, sig_out, codes_in, cot_in, sig_in, grad_out, total_out,
    home_grad, home_total, input_grad, filter_grad,
    cot_spec, send_sem, recv_sem, load_sem, store_sem,
):
    loads = [
        pltpu.make_async_copy(source, target, load_sem.at[index])
        for index, (source, target) in enumerate(
            (
                (codes_hbm, codes), (cotangent_hbm, cotangent), (signal_hbm, signal),
                (first_hbm, first), (turn_hbm, turn), (second_hbm, second),
                (second_back_hbm, second_back), (first_back_hbm, first_back),
                (powers_hbm, powers), (mask_hbm, mask),
            )
        )
    ]
    for load in loads:
        load.start()
    s, d = lax.axis_index("seq"), lax.axis_index("dp")
    me = s * DP + d
    side, core = d // 2, lax.rem(d, 2)
    q = core * 2 + side
    place = q * SEQ + s
    along = [lax.rem(s + step, Z) for step in range(Z)]
    across = [lax.rem(s // Z + step, X) * Z for step in range(X)]
    up = [lax.rem(s // (Z * X) + step, Y) * (Z * X) for step in range(Y)]
    sides = [lax.rem(side + step, 2) for step in range(2)]
    cores = [lax.rem(core + step, 2) for step in range(2)]

    seq_at = {
        (a, b, c): up[a] + across[b] + along[c]
        for a in range(Y) for b in range(X) for c in range(Z)
    }
    first_at = {step: to_seq * DP for step, to_seq in seq_at.items()}
    dp_at = {
        (a, b): (cores[b] * 2 + sides[a], sides[a] * 2 + cores[b])
        for a in range(2) for b in range(2)
    }
    place_at = {near: to_q * SEQ for near, (to_q, _) in dp_at.items()}

    def target(step):
        seq_step, near = step[:3], step[3:]
        to_seq = seq_at[seq_step]
        return to_seq, place_at[near] + to_seq, first_at[seq_step] + dp_at[near][1]

    everyone = [step for step in hops(DP_STEPS) if any(step)]
    barrier = pltpu.get_barrier_semaphore()
    for step in everyone:
        pl.semaphore_signal(barrier, inc=1, device_id=target(step)[2], device_id_type=LOGICAL)

    def post(index, source, destination, other):
        pltpu.make_async_remote_copy(
            src_ref=source, dst_ref=destination,
            send_sem=send_sem.at[index], recv_sem=recv_sem.at[index],
            device_id=other, device_id_type=LOGICAL,
        ).start()

    def drain(index, array, count):
        part = array.at[pl.ds(0, count)]
        return pltpu.make_async_remote_copy(
            src_ref=part, dst_ref=part,
            send_sem=send_sem.at[index], recv_sem=recv_sem.at[index],
            device_id=me, device_id_type=LOGICAL,
        )

    loads[0].wait()
    codes_out[...] = spread(wide, dot_nt(same((SEQ, ALL), q * SEQ), codes[...]), SEQ)
    loads[1].wait()
    eye = same((ALL, ALL))
    cot_out[...] = spread(wide, dot_nt(eye, cotangent[...]), ALL)
    pl.semaphore_wait(barrier, ALL - 1)

    for step in hops(((0, 0),)):
        if any(step):
            to_seq, _, other = target(step)
            post(0, codes_out.at[to_seq], codes_in.at[s], other)
    for step in everyone:
        _, to_place, other = target(step)
        post(1, cot_out.at[to_place], cot_in.at[place], other)

    loads[2].wait()
    sig_out[...] = spread(wide, dot_nt(eye, signal[...]), ALL)
    for step in everyone:
        _, to_place, other = target(step)
        post(2, sig_out.at[to_place], sig_in.at[place], other)
    codes_in[pl.ds(s, 1)] = codes_out[pl.ds(s, 1)]
    cot_in[pl.ds(place, 1)] = cot_out[pl.ds(place, 1)]
    sig_in[pl.ds(place, 1)] = sig_out[pl.ds(place, 1)]
    for load in loads[3:]:
        load.wait()
    unit = jnp.full((1, LANES), exponents[place].astype(F32), F32)
    scale = jnp.exp2(unit) * (2.0 / POINTS)
    direct = skip[place]

    drain(0, codes_in, SEQ - 1).wait_recv()
    wide[pl.ds(0, SEQ)] = codes_in[...].astype(F32)
    (codes_spec,) = forward(gather(wide, 0).astype(BF16), first[...], turn[...], second[...])

    drain(1, cot_in, ALL - 1).wait_recv()
    wide[...] = cot_in[...].astype(F32)
    cots = [gather(wide, index * SEQ) for index in range(DP)]
    spectra = forward(
        jnp.concatenate(cots, axis=1).astype(BF16), first[...], turn[...], second[...]
    )
    for index, spectrum in enumerate(spectra):
        cot_spec[index] = spectrum
    back = backward(
        [conj_product(codes_spec, spectrum) for spectrum in spectra],
        turn[...], second_back[...], first_back[...],
    )
    for index in range(DP):
        grad = back[:, index * LANES : (index + 1) * LANES] * scale + direct * cots[index]
        part = pl.ds(index * SEQ, SEQ)
        for row in range(ROWS):
            wide[part, row, :] = grad[row * SEQ : (row + 1) * SEQ]
        grad_out[part] = wide[part].astype(BF16)
    for step in everyone[:EARLY]:
        _, to_place, other = target(step)
        post(3, grad_out.at[to_place], home_grad.at[place], other)

    drain(2, sig_in, ALL - 1).wait_recv()
    wide[...] = sig_in[...].astype(F32)
    total_spec = jnp.zeros((HALF, 2 * LANES), F32)
    spectra = forward(
        jnp.concatenate([gather(wide, index * SEQ) for index in range(DP)], axis=1).astype(BF16),
        first[...], turn[...], second[...],
    )
    for index, spectrum in enumerate(spectra):
        total_spec += conj_product(spectrum, cot_spec[index])
    total = backward([total_spec], turn[...], second_back[...], first_back[...])
    total = total * (2.0 / POINTS)
    for row in range(ROWS):
        wide[pl.ds(0, SEQ), row, :] = total[row * SEQ : (row + 1) * SEQ]
    total_out[...] = wide[pl.ds(0, SEQ)].astype(BF16)
    for step in hops(((0, 0), (1, 0))):
        if any(step):
            to_seq, _, other = target(step)
            post(4, total_out.at[to_seq], home_total.at[s + side * SEQ], other)
    for step in everyone[EARLY:]:
        _, to_place, other = target(step)
        post(3, grad_out.at[to_place], home_grad.at[place], other)
    home_total[pl.ds(s + side * SEQ, 1)] = total_out[pl.ds(s, 1)]
    home_grad[pl.ds(place, 1)] = grad_out[pl.ds(place, 1)]

    eye = same((LANES, LANES))
    half = 2 * SEQ
    channels = pl.ds(pl.multiple_of(core * half, LANES), half)
    factor = jnp.exp2(powers[...].astype(F32))
    factor = jnp.where(core == 0, factor[:, :half], factor[:, half:])
    drain(4, home_total, half - 1).wait_recv()
    wide[pl.ds(0, half)] = home_total[...].astype(F32)
    for row in range(ROWS):
        part = pl.ds(row * LANES, LANES)
        value = dot_nt(eye, wide[pl.ds(0, half), row, :].astype(BF16))
        filter_grad[part, :] = (mask[part, channels].astype(F32) * factor * value).astype(BF16)
    across_core = pltpu.make_async_remote_copy(
        src_ref=filter_grad, dst_ref=filter_hbm.at[core],
        send_sem=send_sem.at[5], recv_sem=recv_sem.at[5],
        device_id=me + 1 - 2 * core, device_id_type=LOGICAL,
    )
    across_core.start()
    store_filter = pltpu.make_async_copy(filter_grad, filter_hbm.at[core], store_sem.at[1])
    store_filter.start()
    drain(3, home_grad, ALL - 1).wait_recv()
    wide[...] = home_grad[...].astype(F32)
    for row in range(ROWS):
        grad = wide[:, row, :].astype(BF16)
        input_grad[pl.ds(row * LANES, LANES), :] = dot_nt(eye, grad).astype(BF16)
    store_input = pltpu.make_async_copy(input_grad, input_hbm, store_sem.at[0])
    store_input.start()
    drain(0, codes_out, SEQ - 1).wait_send()
    drain(1, cot_out, ALL - 1).wait_send()
    drain(2, sig_out, ALL - 1).wait_send()
    drain(3, grad_out, ALL - 1).wait_send()
    drain(4, home_total, half - 1).wait_send()
    store_filter.wait()
    across_core.wait()
    store_input.wait()


def last_kernel(input_main, filter_main, input_grad, filter_grad, input_held, halves, held, load_sem, store_sem):
    load_halves = [
        pltpu.make_async_copy(filter_main.at[index], halves.at[index], load_sem.at[index])
        for index in range(2)
    ]
    load_input = pltpu.make_async_copy(input_main, input_held, load_sem.at[2])
    for load in load_halves:
        load.start()
    load_input.start()
    for load in load_halves:
        load.wait()
    stores = []
    for row in range(ROWS):
        part = pl.ds(row * LANES, LANES)
        for index in range(2):
            value = halves[index, part, :].astype(F32) * (1.0 / math.sqrt(DP * HALF * LANES))
            held[part, pl.ds(index * LANES, LANES)] = value
        stores.append(
            pltpu.make_async_copy(held.at[part], filter_grad.at[part], store_sem.at[row])
        )
        stores[-1].start()
    load_input.wait()
    store_input = pltpu.make_async_copy(input_held, input_grad, store_sem.at[ROWS])
    store_input.start()
    for store in stores:
        store.wait()
    store_input.wait()


def per_device(signal, cotangent, filter_codes, keep_mask, exponents, skip):
    span, width = signal.shape[1], signal.shape[2]
    smem = pl.BlockSpec(memory_space=pltpu.SMEM)
    hbm = pl.BlockSpec(memory_space=pltpu.HBM)
    constants = [jnp.asarray(table) for table in tables()]
    message = (ROWS, LANES)
    results = (
        jax.ShapeDtypeStruct((span, width), BF16),
        jax.ShapeDtypeStruct((span, width), F32),
    )
    input_main, filter_main = pl.pallas_call(
        main_kernel,
        out_shape=(results[0], jax.ShapeDtypeStruct((2, span, width // 2), BF16)),
        in_specs=[hbm] * 4 + [smem] * 2 + [hbm] * 6,
        out_specs=(hbm, hbm),
        scratch_shapes=[
            pltpu.VMEM((span, width), BF16),
            pltpu.VMEM((span, width), BF16),
            pltpu.VMEM((span, width), BF16),
            pltpu.VMEM((span, width), jnp.int32),
            pltpu.VMEM((1, width), jnp.int32),
            *[pltpu.VMEM(table.shape, table.dtype) for table in constants],
            pltpu.VMEM((ALL,) + message, F32),
            pltpu.VMEM((SEQ,) + message, BF16),
            pltpu.VMEM((ALL,) + message, BF16),
            pltpu.VMEM((ALL,) + message, BF16),
            pltpu.VMEM((SEQ,) + message, BF16),
            pltpu.VMEM((ALL,) + message, BF16),
            pltpu.VMEM((ALL,) + message, BF16),
            pltpu.VMEM((ALL,) + message, BF16),
            pltpu.VMEM((SEQ,) + message, BF16),
            pltpu.VMEM((ALL,) + message, BF16),
            pltpu.VMEM((2 * SEQ,) + message, BF16),
            pltpu.VMEM((span, width), BF16),
            pltpu.VMEM((span, width // 2), BF16),
            pltpu.VMEM((DP, HALF, 2 * LANES), F32),
            pltpu.SemaphoreType.DMA((6,)),
            pltpu.SemaphoreType.DMA((6,)),
            pltpu.SemaphoreType.DMA((10,)),
            pltpu.SemaphoreType.DMA((2,)),
        ],
        compiler_params=pltpu.CompilerParams(
            collective_id=0, has_side_effects=True, vmem_limit_bytes=VMEM_LIMIT
        ),
        name="main",
    )(
        signal.reshape(span, width), cotangent.reshape(span, width), filter_codes, keep_mask,
        exponents, skip, exponents.reshape(1, width), *constants,
    )
    input_grad, filter_grad = pl.pallas_call(
        last_kernel,
        out_shape=results,
        in_specs=[hbm, hbm],
        out_specs=(hbm, hbm),
        scratch_shapes=[
            pltpu.VMEM((span, width), BF16),
            pltpu.VMEM((2, span, width // 2), BF16),
            pltpu.VMEM((span, width), F32),
            pltpu.SemaphoreType.DMA((3,)),
            pltpu.SemaphoreType.DMA((ROWS + 1,)),
        ],
        compiler_params=pltpu.CompilerParams(vmem_limit_bytes=VMEM_LIMIT),
        name="last",
    )(input_main, filter_main)
    return input_grad.reshape(signal.shape), filter_grad


def solution(mesh):
    return jax.shard_map(
        per_device,
        mesh=mesh,
        in_specs=(
            P("dp", "seq", None),
            P("dp", "seq", None),
            P("seq", None),
            P("seq", None),
            P(),
            P(),
        ),
        out_specs=(P("dp", "seq", None), P("seq", None)),
        check_vma=False,
    )
```

```python
import functools
import math

import jax
import jax.numpy as jnp
import numpy as np
from jax import lax
from jax.experimental import pallas as pl
from jax.experimental.pallas import tpu as pltpu
from jax.sharding import PartitionSpec as P

LOGICAL = pl.DeviceIdType.LOGICAL
F32 = jnp.float32
BF16 = jnp.bfloat16
LANES = 128
ROWS = 4
SEQ = 64
DP = 4
ALL = SEQ * DP
HALF = SEQ * ROWS
POINTS = 2 * HALF * LANES
Z, X, Y = 8, 4, 2
VMEM_LIMIT = 58 << 20


def split(values):
    high = values.astype(BF16)
    return high, (values - high.astype(F32)).astype(BF16)


def np_split(values):
    values = values.astype(np.float32)
    high = values.astype(jnp.bfloat16)
    return high, (values - high.astype(np.float32)).astype(jnp.bfloat16)


def tables():
    rows = (ROWS * np.arange(SEQ)[None, :] + np.arange(ROWS)[:, None]).reshape(-1)
    odd = 2 * np.arange(HALF) + 1
    angle = 2 * np.pi / (4 * HALF) * ((odd[:, None] * rows[None, :]) % (4 * HALF))
    first = np.concatenate([np.cos(angle), -np.sin(angle)], axis=0)
    lane = np.arange(LANES)
    angle = 2 * np.pi / (2 * POINTS) * ((odd[:, None] * lane[None, :]) % (2 * POINTS))
    turn = np.concatenate([np.cos(angle), -np.sin(angle)], axis=1).astype(np.float32)
    angle = 2 * np.pi / LANES * ((lane[:, None] * lane[None, :]) % LANES)
    cos, sin = np.cos(angle), np.sin(angle)
    second = np.block([[cos, -sin], [sin, cos]])
    first_high, first_low = np_split(first)
    second_high, second_low = np_split(second)
    return (
        np.concatenate([first_high, first_low], axis=1),
        turn,
        np.concatenate([second_high, second_high, second_low], axis=0),
        np.concatenate([second_high.T, second_high.T, second_low.T], axis=0),
        np.concatenate([first_high.T, first_low.T, first_high.T], axis=1),
    )


def dot(left, right):
    return jnp.dot(left, right, preferred_element_type=F32)


def dot_nt(left, right):
    return lax.dot_general(left, right, (((1,), (1,)), ((), ())), preferred_element_type=F32)


def same(shape, offset=0, factor=1):
    row = lax.broadcasted_iota(jnp.int32, shape, 0)
    column = lax.broadcasted_iota(jnp.int32, shape, 1)
    return jnp.where(column == factor * row + offset, 1.0, 0.0).astype(BF16)


def mix(values, matrix):
    high, low = split(values)
    return dot(jnp.concatenate([high, low, high], axis=1), matrix)


def forward(rows, first, turn, second):
    both = dot(first, jnp.concatenate([rows, rows], axis=0))
    cos, sin = turn[:, :LANES], turn[:, LANES:]
    spectra = []
    for at in range(0, rows.shape[1], LANES):
        real, imag = both[:HALF, at : at + LANES], both[HALF:, at : at + LANES]
        turned = jnp.concatenate([real * cos - imag * sin, real * sin + imag * cos], axis=1)
        spectra.append(mix(turned, second))
    return spectra


def backward(spectra, turn, second_back, first_back):
    cos, sin = turn[:, :LANES], turn[:, LANES:]
    columns = []
    for spectrum in spectra:
        both = mix(spectrum, second_back)
        real, imag = both[:, :LANES], both[:, LANES:]
        columns.append(
            jnp.concatenate([real * cos + imag * sin, imag * cos - real * sin], axis=0)
        )
    high, low = split(jnp.concatenate(columns, axis=1))
    return dot(first_back, jnp.concatenate([high, high, low], axis=0))


def conj_product(left, right):
    left_real, left_imag = left[:, :LANES], left[:, LANES:]
    right_real, right_imag = right[:, :LANES], right[:, LANES:]
    return jnp.concatenate(
        [
            left_real * right_real + left_imag * right_imag,
            left_real * right_imag - left_imag * right_real,
        ],
        axis=1,
    )


EARLY = 191
DP_STEPS = ((1, 1), (1, 0), (0, 1), (0, 0))


def hops(near):
    def distance(step):
        up, across, along, side, _ = step
        turns = min(across, X - across) + ((0, 1), (2, 1))[up][side]
        return 2 * turns + min(along, Z - along)

    steps = [
        (up, across, along, side, core)
        for along in range(Z)
        for across in range(X)
        for up in range(Y)
        for side, core in near
    ]
    steps.sort(key=lambda step: -distance(step))
    return steps


def spread(wide, values, count):
    for row in range(ROWS):
        wide[pl.ds(0, count), row, :] = values[:, row * LANES : (row + 1) * LANES]
    return wide[pl.ds(0, count)].astype(BF16)


def gather(wide, start):
    return jnp.concatenate([wide[pl.ds(start, SEQ), row, :] for row in range(ROWS)], axis=0)


def main_kernel(
    signal_hbm, cotangent_hbm, codes_hbm, mask_hbm, exponents, skip, powers_hbm,
    first_hbm, turn_hbm, second_hbm, second_back_hbm, first_back_hbm,
    input_main, filter_main,
    signal, cotangent, codes, mask, powers, first, turn, second, second_back, first_back,
    wide, codes_out, cot_out, sig_out, codes_in, cot_in, sig_in, grad_out, total_out,
    home_grad, home_total,
    cot_spec, send_sem, recv_sem, load_sem,
):
    loads = [
        pltpu.make_async_copy(source, target, load_sem.at[index])
        for index, (source, target) in enumerate(
            (
                (codes_hbm, codes), (cotangent_hbm, cotangent), (signal_hbm, signal),
                (first_hbm, first), (turn_hbm, turn), (second_hbm, second),
                (second_back_hbm, second_back), (first_back_hbm, first_back),
                (powers_hbm, powers), (mask_hbm, mask),
            )
        )
    ]
    for load in loads:
        load.start()
    s, d = lax.axis_index("seq"), lax.axis_index("dp")
    me = s * DP + d
    side, core = d // 2, lax.rem(d, 2)
    q = core * 2 + side
    place = q * SEQ + s
    along = [lax.rem(s + step, Z) for step in range(Z)]
    across = [lax.rem(s // Z + step, X) * Z for step in range(X)]
    up = [lax.rem(s // (Z * X) + step, Y) * (Z * X) for step in range(Y)]
    sides = [lax.rem(side + step, 2) for step in range(2)]
    cores = [lax.rem(core + step, 2) for step in range(2)]

    seq_at = {
        (a, b, c): up[a] + across[b] + along[c]
        for a in range(Y) for b in range(X) for c in range(Z)
    }
    first_at = {step: to_seq * DP for step, to_seq in seq_at.items()}
    dp_at = {
        (a, b): (cores[b] * 2 + sides[a], sides[a] * 2 + cores[b])
        for a in range(2) for b in range(2)
    }
    place_at = {near: to_q * SEQ for near, (to_q, _) in dp_at.items()}

    def target(step):
        seq_step, near = step[:3], step[3:]
        to_seq = seq_at[seq_step]
        return to_seq, place_at[near] + to_seq, first_at[seq_step] + dp_at[near][1]

    everyone = [step for step in hops(DP_STEPS) if any(step)]
    barrier = pltpu.get_barrier_semaphore()
    for step in everyone:
        pl.semaphore_signal(barrier, inc=1, device_id=target(step)[2], device_id_type=LOGICAL)

    def post(index, source, destination, other):
        pltpu.make_async_remote_copy(
            src_ref=source, dst_ref=destination,
            send_sem=send_sem.at[index], recv_sem=recv_sem.at[index],
            device_id=other, device_id_type=LOGICAL,
        ).start()

    def drain(index, array, count):
        part = array.at[pl.ds(0, count)]
        return pltpu.make_async_remote_copy(
            src_ref=part, dst_ref=part,
            send_sem=send_sem.at[index], recv_sem=recv_sem.at[index],
            device_id=me, device_id_type=LOGICAL,
        )

    loads[0].wait()
    codes_out[...] = spread(wide, dot_nt(same((SEQ, ALL), q * SEQ), codes[...]), SEQ)
    loads[1].wait()
    eye = same((ALL, ALL))
    cot_out[...] = spread(wide, dot_nt(eye, cotangent[...]), ALL)
    pl.semaphore_wait(barrier, ALL - 1)

    for step in hops(((0, 0),)):
        if any(step):
            to_seq, _, other = target(step)
            post(0, codes_out.at[to_seq], codes_in.at[s], other)
    for step in everyone:
        _, to_place, other = target(step)
        post(1, cot_out.at[to_place], cot_in.at[place], other)

    loads[2].wait()
    sig_out[...] = spread(wide, dot_nt(eye, signal[...]), ALL)
    for step in everyone:
        _, to_place, other = target(step)
        post(2, sig_out.at[to_place], sig_in.at[place], other)
    codes_in[pl.ds(s, 1)] = codes_out[pl.ds(s, 1)]
    cot_in[pl.ds(place, 1)] = cot_out[pl.ds(place, 1)]
    sig_in[pl.ds(place, 1)] = sig_out[pl.ds(place, 1)]
    for load in loads[3:]:
        load.wait()
    unit = jnp.full((1, LANES), exponents[place].astype(F32), F32)
    scale = jnp.exp2(unit) * (2.0 / POINTS)
    direct = skip[place]

    drain(0, codes_in, SEQ - 1).wait_recv()
    wide[pl.ds(0, SEQ)] = codes_in[...].astype(F32)
    (codes_spec,) = forward(gather(wide, 0).astype(BF16), first[...], turn[...], second[...])

    drain(1, cot_in, ALL - 1).wait_recv()
    wide[...] = cot_in[...].astype(F32)
    cots = [gather(wide, index * SEQ) for index in range(DP)]
    spectra = forward(
        jnp.concatenate(cots, axis=1).astype(BF16), first[...], turn[...], second[...]
    )
    for index, spectrum in enumerate(spectra):
        cot_spec[index] = spectrum
    back = backward(
        [conj_product(codes_spec, spectrum) for spectrum in spectra],
        turn[...], second_back[...], first_back[...],
    )
    for index in range(DP):
        grad = back[:, index * LANES : (index + 1) * LANES] * scale + direct * cots[index]
        part = pl.ds(index * SEQ, SEQ)
        for row in range(ROWS):
            wide[part, row, :] = grad[row * SEQ : (row + 1) * SEQ]
        grad_out[part] = wide[part].astype(BF16)
    for step in everyone[:EARLY]:
        _, to_place, other = target(step)
        post(3, grad_out.at[to_place], home_grad.at[place], other)

    drain(2, sig_in, ALL - 1).wait_recv()
    wide[...] = sig_in[...].astype(F32)
    total_spec = jnp.zeros((HALF, 2 * LANES), F32)
    spectra = forward(
        jnp.concatenate([gather(wide, index * SEQ) for index in range(DP)], axis=1).astype(BF16),
        first[...], turn[...], second[...],
    )
    for index, spectrum in enumerate(spectra):
        total_spec += conj_product(spectrum, cot_spec[index])
    total = backward([total_spec], turn[...], second_back[...], first_back[...])
    total = total * (2.0 / POINTS)
    for row in range(ROWS):
        wide[pl.ds(0, SEQ), row, :] = total[row * SEQ : (row + 1) * SEQ]
    total_out[...] = wide[pl.ds(0, SEQ)].astype(BF16)
    for step in hops(((0, 0), (1, 0))):
        if any(step):
            to_seq, _, other = target(step)
            post(4, total_out.at[to_seq], home_total.at[s + side * SEQ], other)
    for step in everyone[EARLY:]:
        _, to_place, other = target(step)
        post(3, grad_out.at[to_place], home_grad.at[place], other)
    home_total[pl.ds(s + side * SEQ, 1)] = total_out[pl.ds(s, 1)]
    home_grad[pl.ds(place, 1)] = grad_out[pl.ds(place, 1)]

    eye = same((LANES, LANES))
    half = 2 * SEQ
    channels = pl.ds(pl.multiple_of(core * half, LANES), half)
    factor = jnp.exp2(powers[...].astype(F32))
    factor = jnp.where(core == 0, factor[:, :half], factor[:, half:])
    drain(4, home_total, half - 1).wait_recv()
    wide[pl.ds(0, half)] = home_total[...].astype(F32)
    for row in range(ROWS):
        part = pl.ds(row * LANES, LANES)
        value = dot_nt(eye, wide[pl.ds(0, half), row, :].astype(BF16))
        value = mask[part, channels].astype(F32) * factor * value
        filter_main[core, part, :] = value.astype(BF16)
    across_core = pltpu.make_async_remote_copy(
        src_ref=filter_main.at[core], dst_ref=filter_main.at[core],
        send_sem=send_sem.at[5], recv_sem=recv_sem.at[5],
        device_id=me + 1 - 2 * core, device_id_type=LOGICAL,
    )
    across_core.start()
    drain(3, home_grad, ALL - 1).wait_recv()
    wide[...] = home_grad[...].astype(F32)
    for row in range(ROWS):
        grad = wide[:, row, :].astype(BF16)
        input_main[pl.ds(row * LANES, LANES), :] = dot_nt(eye, grad).astype(BF16)
    drain(0, codes_out, SEQ - 1).wait_send()
    drain(1, cot_out, ALL - 1).wait_send()
    drain(2, sig_out, ALL - 1).wait_send()
    drain(3, grad_out, ALL - 1).wait_send()
    drain(4, home_total, half - 1).wait_send()
    across_core.wait()


def last_kernel(input_main, filter_main, input_grad, filter_grad, held, sem):
    stores = [pltpu.make_async_copy(input_main, input_grad, sem.at[ROWS])]
    stores[0].start()
    for row in range(ROWS):
        part = pl.ds(row * LANES, LANES)
        for index in range(2):
            value = filter_main[index, part, :].astype(F32) * (1.0 / math.sqrt(DP * HALF * LANES))
            held[part, pl.ds(index * LANES, LANES)] = value
        stores.append(pltpu.make_async_copy(held.at[part], filter_grad.at[part], sem.at[row]))
        stores[-1].start()
    for store in stores:
        store.wait()


def per_device(signal, cotangent, filter_codes, keep_mask, exponents, skip):
    span, width = signal.shape[1], signal.shape[2]
    smem = pl.BlockSpec(memory_space=pltpu.SMEM)
    hbm = pl.BlockSpec(memory_space=pltpu.HBM)
    vmem = pl.BlockSpec(memory_space=pltpu.VMEM)
    constants = [jnp.asarray(table) for table in tables()]
    message = (ROWS, LANES)
    results = (
        jax.ShapeDtypeStruct((span, width), BF16),
        jax.ShapeDtypeStruct((span, width), F32),
    )
    input_main, filter_main = pl.pallas_call(
        main_kernel,
        out_shape=(pltpu.VMEM((span, width), BF16), pltpu.VMEM((2, span, width // 2), BF16)),
        in_specs=[hbm] * 4 + [smem] * 2 + [hbm] * 6,
        out_specs=(vmem, vmem),
        scratch_shapes=[
            pltpu.VMEM((span, width), BF16),
            pltpu.VMEM((span, width), BF16),
            pltpu.VMEM((span, width), BF16),
            pltpu.VMEM((span, width), jnp.int32),
            pltpu.VMEM((1, width), jnp.int32),
            *[pltpu.VMEM(table.shape, table.dtype) for table in constants],
            pltpu.VMEM((ALL,) + message, F32),
            pltpu.VMEM((SEQ,) + message, BF16),
            pltpu.VMEM((ALL,) + message, BF16),
            pltpu.VMEM((ALL,) + message, BF16),
            pltpu.VMEM((SEQ,) + message, BF16),
            pltpu.VMEM((ALL,) + message, BF16),
            pltpu.VMEM((ALL,) + message, BF16),
            pltpu.VMEM((ALL,) + message, BF16),
            pltpu.VMEM((SEQ,) + message, BF16),
            pltpu.VMEM((ALL,) + message, BF16),
            pltpu.VMEM((2 * SEQ,) + message, BF16),
            pltpu.VMEM((DP, HALF, 2 * LANES), F32),
            pltpu.SemaphoreType.DMA((6,)),
            pltpu.SemaphoreType.DMA((6,)),
            pltpu.SemaphoreType.DMA((10,)),
        ],
        compiler_params=pltpu.CompilerParams(
            collective_id=0, has_side_effects=True, vmem_limit_bytes=VMEM_LIMIT
        ),
        name="main",
    )(
        signal.reshape(span, width), cotangent.reshape(span, width), filter_codes, keep_mask,
        exponents, skip, exponents.reshape(1, width), *constants,
    )
    input_grad, filter_grad = pl.pallas_call(
        last_kernel,
        out_shape=results,
        in_specs=[vmem, vmem],
        out_specs=(hbm, hbm),
        scratch_shapes=[
            pltpu.VMEM((span, width), F32),
            pltpu.SemaphoreType.DMA((ROWS + 1,)),
        ],
        compiler_params=pltpu.CompilerParams(vmem_limit_bytes=4 << 20),
        name="last",
    )(input_main, filter_main)
    return input_grad.reshape(signal.shape), filter_grad


def solution(mesh):
    return jax.shard_map(
        per_device,
        mesh=mesh,
        in_specs=(
            P("dp", "seq", None),
            P("dp", "seq", None),
            P("seq", None),
            P("seq", None),
            P(),
            P(),
        ),
        out_specs=(P("dp", "seq", None), P("seq", None)),
        check_vma=False,
    )
```

```python
import functools
import math

import jax
import jax.numpy as jnp
import numpy as np
from jax import lax
from jax.experimental import pallas as pl
from jax.experimental.pallas import tpu as pltpu
from jax.sharding import PartitionSpec as P

LOGICAL = pl.DeviceIdType.LOGICAL
F32 = jnp.float32
BF16 = jnp.bfloat16
LANES = 128
ROWS = 4
SEQ = 64
DP = 4
ALL = SEQ * DP
HALF = SEQ * ROWS
POINTS = 2 * HALF * LANES
Z, X, Y = 8, 4, 2
VMEM_LIMIT = 58 << 20


def split(values):
    high = values.astype(BF16)
    return high, (values - high.astype(F32)).astype(BF16)


def np_split(values):
    values = values.astype(np.float32)
    high = values.astype(jnp.bfloat16)
    return high, (values - high.astype(np.float32)).astype(jnp.bfloat16)


def tables():
    rows = (ROWS * np.arange(SEQ)[None, :] + np.arange(ROWS)[:, None]).reshape(-1)
    odd = 2 * np.arange(HALF) + 1
    angle = 2 * np.pi / (4 * HALF) * ((odd[:, None] * rows[None, :]) % (4 * HALF))
    first = np.concatenate([np.cos(angle), -np.sin(angle)], axis=0)
    lane = np.arange(LANES)
    angle = 2 * np.pi / (2 * POINTS) * ((odd[:, None] * lane[None, :]) % (2 * POINTS))
    turn = np.concatenate([np.cos(angle), -np.sin(angle)], axis=1).astype(np.float32)
    angle = 2 * np.pi / LANES * ((lane[:, None] * lane[None, :]) % LANES)
    cos, sin = np.cos(angle), np.sin(angle)
    second = np.block([[cos, -sin], [sin, cos]])
    first_high, first_low = np_split(first)
    second_high, second_low = np_split(second)
    return (
        np.concatenate([first_high, first_low], axis=1),
        turn,
        np.concatenate([second_high, second_high, second_low], axis=0),
        np.concatenate([second_high.T, second_high.T, second_low.T], axis=0),
        np.concatenate([first_high.T, first_low.T, first_high.T], axis=1),
    )


def dot(left, right):
    return jnp.dot(left, right, preferred_element_type=F32)


def dot_nt(left, right):
    return lax.dot_general(left, right, (((1,), (1,)), ((), ())), preferred_element_type=F32)


def same(shape, offset=0, factor=1):
    row = lax.broadcasted_iota(jnp.int32, shape, 0)
    column = lax.broadcasted_iota(jnp.int32, shape, 1)
    return jnp.where(column == factor * row + offset, 1.0, 0.0).astype(BF16)


def mix(values, matrix):
    high, low = split(values)
    return dot(jnp.concatenate([high, low, high], axis=1), matrix)


def forward(rows, first, turn, second):
    both = dot(first, jnp.concatenate([rows, rows], axis=0))
    cos, sin = turn[:, :LANES], turn[:, LANES:]
    spectra = []
    for at in range(0, rows.shape[1], LANES):
        real, imag = both[:HALF, at : at + LANES], both[HALF:, at : at + LANES]
        turned = jnp.concatenate([real * cos - imag * sin, real * sin + imag * cos], axis=1)
        spectra.append(mix(turned, second))
    return spectra


def backward(spectra, turn, second_back, first_back):
    cos, sin = turn[:, :LANES], turn[:, LANES:]
    columns = []
    for spectrum in spectra:
        both = mix(spectrum, second_back)
        real, imag = both[:, :LANES], both[:, LANES:]
        columns.append(
            jnp.concatenate([real * cos + imag * sin, imag * cos - real * sin], axis=0)
        )
    high, low = split(jnp.concatenate(columns, axis=1))
    return dot(first_back, jnp.concatenate([high, high, low], axis=0))


def conj_product(left, right):
    left_real, left_imag = left[:, :LANES], left[:, LANES:]
    right_real, right_imag = right[:, :LANES], right[:, LANES:]
    return jnp.concatenate(
        [
            left_real * right_real + left_imag * right_imag,
            left_real * right_imag - left_imag * right_real,
        ],
        axis=1,
    )


EARLY = 191
DP_STEPS = ((1, 1), (1, 0), (0, 1), (0, 0))


def hops(near, weight):
    def distance(step):
        up, across, along, side, _ = step
        turns = min(across, X - across) + ((0, 1), (2, 1))[up][side]
        return weight * turns + min(along, Z - along)

    steps = [
        (up, across, along, side, core)
        for along in range(Z)
        for across in range(X)
        for up in range(Y)
        for side, core in near
    ]
    steps.sort(key=lambda step: -distance(step))
    return steps


def spread(wide, values, count):
    for row in range(ROWS):
        wide[pl.ds(0, count), row, :] = values[:, row * LANES : (row + 1) * LANES]
    return wide[pl.ds(0, count)].astype(BF16)


def gather(wide, start):
    return jnp.concatenate([wide[pl.ds(start, SEQ), row, :] for row in range(ROWS)], axis=0)


def main_kernel(
    signal_hbm, cotangent_hbm, codes_hbm, mask_hbm, exponents, skip, powers_hbm,
    first_hbm, turn_hbm, second_hbm, second_back_hbm, first_back_hbm,
    input_main, filter_main,
    signal, cotangent, codes, mask, powers, first, turn, second, second_back, first_back,
    wide, codes_out, cot_out, sig_out, codes_in, cot_in, sig_in, grad_out, total_out,
    home_grad, home_total,
    cot_spec, send_sem, recv_sem, load_sem,
):
    loads = [
        pltpu.make_async_copy(source, target, load_sem.at[index])
        for index, (source, target) in enumerate(
            (
                (codes_hbm, codes), (cotangent_hbm, cotangent), (signal_hbm, signal),
                (first_hbm, first), (turn_hbm, turn), (second_hbm, second),
                (second_back_hbm, second_back), (first_back_hbm, first_back),
                (powers_hbm, powers), (mask_hbm, mask),
            )
        )
    ]
    for load in loads:
        load.start()
    s, d = lax.axis_index("seq"), lax.axis_index("dp")
    me = s * DP + d
    side, core = d // 2, lax.rem(d, 2)
    q = core * 2 + side
    place = q * SEQ + s
    along = [lax.rem(s + step, Z) for step in range(Z)]
    across = [lax.rem(s // Z + step, X) * Z for step in range(X)]
    up = [lax.rem(s // (Z * X) + step, Y) * (Z * X) for step in range(Y)]
    sides = [lax.rem(side + step, 2) for step in range(2)]
    cores = [lax.rem(core + step, 2) for step in range(2)]

    seq_at = {
        (a, b, c): up[a] + across[b] + along[c]
        for a in range(Y) for b in range(X) for c in range(Z)
    }
    first_at = {step: to_seq * DP for step, to_seq in seq_at.items()}
    dp_at = {
        (a, b): (cores[b] * 2 + sides[a], sides[a] * 2 + cores[b])
        for a in range(2) for b in range(2)
    }
    place_at = {near: to_q * SEQ for near, (to_q, _) in dp_at.items()}

    def target(step):
        seq_step, near = step[:3], step[3:]
        to_seq = seq_at[seq_step]
        return to_seq, place_at[near] + to_seq, first_at[seq_step] + dp_at[near][1]

    everyone = [step for step in hops(DP_STEPS, 1.5) if any(step)]
    barrier = pltpu.get_barrier_semaphore()
    for step in hops(DP_STEPS, 1)[: ALL - 1]:
        pl.semaphore_signal(barrier, inc=1, device_id=target(step)[2], device_id_type=LOGICAL)

    def post(index, source, destination, other):
        pltpu.make_async_remote_copy(
            src_ref=source, dst_ref=destination,
            send_sem=send_sem.at[index], recv_sem=recv_sem.at[index],
            device_id=other, device_id_type=LOGICAL,
        ).start()

    def drain(index, array, count):
        part = array.at[pl.ds(0, count)]
        return pltpu.make_async_remote_copy(
            src_ref=part, dst_ref=part,
            send_sem=send_sem.at[index], recv_sem=recv_sem.at[index],
            device_id=me, device_id_type=LOGICAL,
        )

    loads[0].wait()
    codes_out[...] = spread(wide, dot_nt(same((SEQ, ALL), q * SEQ), codes[...]), SEQ)
    loads[1].wait()
    eye = same((ALL, ALL))
    cot_out[...] = spread(wide, dot_nt(eye, cotangent[...]), ALL)
    pl.semaphore_wait(barrier, ALL - 1)

    for step in hops(((0, 0),), 1.5):
        if any(step):
            to_seq, _, other = target(step)
            post(0, codes_out.at[to_seq], codes_in.at[s], other)
    for step in everyone:
        _, to_place, other = target(step)
        post(1, cot_out.at[to_place], cot_in.at[place], other)

    loads[2].wait()
    sig_out[...] = spread(wide, dot_nt(eye, signal[...]), ALL)
    for step in everyone:
        _, to_place, other = target(step)
        post(2, sig_out.at[to_place], sig_in.at[place], other)
    codes_in[pl.ds(s, 1)] = codes_out[pl.ds(s, 1)]
    cot_in[pl.ds(place, 1)] = cot_out[pl.ds(place, 1)]
    sig_in[pl.ds(place, 1)] = sig_out[pl.ds(place, 1)]
    for load in loads[3:]:
        load.wait()
    unit = jnp.full((1, LANES), exponents[place].astype(F32), F32)
    scale = jnp.exp2(unit) * (2.0 / POINTS)
    direct = skip[place]

    drain(0, codes_in, SEQ - 1).wait_recv()
    wide[pl.ds(0, SEQ)] = codes_in[...].astype(F32)
    (codes_spec,) = forward(gather(wide, 0).astype(BF16), first[...], turn[...], second[...])

    drain(1, cot_in, ALL - 1).wait_recv()
    wide[...] = cot_in[...].astype(F32)
    cots = [gather(wide, index * SEQ) for index in range(DP)]
    spectra = forward(
        jnp.concatenate(cots, axis=1).astype(BF16), first[...], turn[...], second[...]
    )
    for index, spectrum in enumerate(spectra):
        cot_spec[index] = spectrum
    back = backward(
        [conj_product(codes_spec, spectrum) for spectrum in spectra],
        turn[...], second_back[...], first_back[...],
    )
    for index in range(DP):
        grad = back[:, index * LANES : (index + 1) * LANES] * scale + direct * cots[index]
        part = pl.ds(index * SEQ, SEQ)
        for row in range(ROWS):
            wide[part, row, :] = grad[row * SEQ : (row + 1) * SEQ]
        grad_out[part] = wide[part].astype(BF16)
    for step in everyone[:EARLY]:
        _, to_place, other = target(step)
        post(3, grad_out.at[to_place], home_grad.at[place], other)

    drain(2, sig_in, ALL - 1).wait_recv()
    wide[...] = sig_in[...].astype(F32)
    total_spec = jnp.zeros((HALF, 2 * LANES), F32)
    spectra = forward(
        jnp.concatenate([gather(wide, index * SEQ) for index in range(DP)], axis=1).astype(BF16),
        first[...], turn[...], second[...],
    )
    for index, spectrum in enumerate(spectra):
        total_spec += conj_product(spectrum, cot_spec[index])
    total = backward([total_spec], turn[...], second_back[...], first_back[...])
    total = total * (2.0 / POINTS)
    for row in range(ROWS):
        wide[pl.ds(0, SEQ), row, :] = total[row * SEQ : (row + 1) * SEQ]
    total_out[...] = wide[pl.ds(0, SEQ)].astype(BF16)
    for step in hops(((0, 0), (1, 0)), 1.5):
        if any(step):
            to_seq, _, other = target(step)
            post(4, total_out.at[to_seq], home_total.at[s + side * SEQ], other)
    for step in everyone[EARLY:]:
        _, to_place, other = target(step)
        post(3, grad_out.at[to_place], home_grad.at[place], other)
    home_total[pl.ds(s + side * SEQ, 1)] = total_out[pl.ds(s, 1)]
    home_grad[pl.ds(place, 1)] = grad_out[pl.ds(place, 1)]

    half = 2 * SEQ
    channels = pl.ds(pl.multiple_of(core * half, LANES), half)
    factor = jnp.exp2(powers[...].astype(F32))
    factor = jnp.where(core == 0, factor[:, :half], factor[:, half:])
    drain(4, home_total, half - 1).wait_recv()
    wide[pl.ds(0, half)] = home_total[...].astype(F32)
    for row in range(ROWS):
        part = pl.ds(row * LANES, LANES)
        value = wide[pl.ds(0, half), row, :].T
        value = mask[part, channels].astype(F32) * factor * value
        filter_main[core, part, :] = value.astype(BF16)
    across_core = pltpu.make_async_remote_copy(
        src_ref=filter_main.at[core], dst_ref=filter_main.at[core],
        send_sem=send_sem.at[5], recv_sem=recv_sem.at[5],
        device_id=me + 1 - 2 * core, device_id_type=LOGICAL,
    )
    across_core.start()
    drain(3, home_grad, ALL - 1).wait_recv()
    wide[...] = home_grad[...].astype(F32)
    for row in range(ROWS):
        input_main[pl.ds(row * LANES, LANES), :] = wide[:, row, :].T.astype(BF16)
    drain(0, codes_out, SEQ - 1).wait_send()
    drain(1, cot_out, ALL - 1).wait_send()
    drain(2, sig_out, ALL - 1).wait_send()
    drain(3, grad_out, ALL - 1).wait_send()
    drain(4, home_total, half - 1).wait_send()
    across_core.wait()


def last_kernel(input_main, filter_main, input_grad, filter_grad, held, sem):
    stores = [pltpu.make_async_copy(input_main, input_grad, sem.at[ROWS])]
    stores[0].start()
    for row in range(ROWS):
        part = pl.ds(row * LANES, LANES)
        for index in range(2):
            value = filter_main[index, part, :].astype(F32) * (1.0 / math.sqrt(DP * HALF * LANES))
            held[part, pl.ds(index * LANES, LANES)] = value
        stores.append(pltpu.make_async_copy(held.at[part], filter_grad.at[part], sem.at[row]))
        stores[-1].start()
    for store in stores:
        store.wait()


def per_device(signal, cotangent, filter_codes, keep_mask, exponents, skip):
    span, width = signal.shape[1], signal.shape[2]
    smem = pl.BlockSpec(memory_space=pltpu.SMEM)
    hbm = pl.BlockSpec(memory_space=pltpu.HBM)
    vmem = pl.BlockSpec(memory_space=pltpu.VMEM)
    constants = [jnp.asarray(table) for table in tables()]
    message = (ROWS, LANES)
    results = (
        jax.ShapeDtypeStruct((span, width), BF16),
        jax.ShapeDtypeStruct((span, width), F32),
    )
    input_main, filter_main = pl.pallas_call(
        main_kernel,
        out_shape=(pltpu.VMEM((span, width), BF16), pltpu.VMEM((2, span, width // 2), BF16)),
        in_specs=[hbm] * 4 + [smem] * 2 + [hbm] * 6,
        out_specs=(vmem, vmem),
        scratch_shapes=[
            pltpu.VMEM((span, width), BF16),
            pltpu.VMEM((span, width), BF16),
            pltpu.VMEM((span, width), BF16),
            pltpu.VMEM((span, width), jnp.int32),
            pltpu.VMEM((1, width), jnp.int32),
            *[pltpu.VMEM(table.shape, table.dtype) for table in constants],
            pltpu.VMEM((ALL,) + message, F32),
            pltpu.VMEM((SEQ,) + message, BF16),
            pltpu.VMEM((ALL,) + message, BF16),
            pltpu.VMEM((ALL,) + message, BF16),
            pltpu.VMEM((SEQ,) + message, BF16),
            pltpu.VMEM((ALL,) + message, BF16),
            pltpu.VMEM((ALL,) + message, BF16),
            pltpu.VMEM((ALL,) + message, BF16),
            pltpu.VMEM((SEQ,) + message, BF16),
            pltpu.VMEM((ALL,) + message, BF16),
            pltpu.VMEM((2 * SEQ,) + message, BF16),
            pltpu.VMEM((DP, HALF, 2 * LANES), F32),
            pltpu.SemaphoreType.DMA((6,)),
            pltpu.SemaphoreType.DMA((6,)),
            pltpu.SemaphoreType.DMA((10,)),
        ],
        compiler_params=pltpu.CompilerParams(
            collective_id=0, has_side_effects=True, vmem_limit_bytes=VMEM_LIMIT
        ),
        name="main",
    )(
        signal.reshape(span, width), cotangent.reshape(span, width), filter_codes, keep_mask,
        exponents, skip, exponents.reshape(1, width), *constants,
    )
    input_grad, filter_grad = pl.pallas_call(
        last_kernel,
        out_shape=results,
        in_specs=[vmem, vmem],
        out_specs=(hbm, hbm),
        scratch_shapes=[
            pltpu.VMEM((span, width), F32),
            pltpu.SemaphoreType.DMA((ROWS + 1,)),
        ],
        compiler_params=pltpu.CompilerParams(vmem_limit_bytes=4 << 20),
        name="last",
    )(input_main, filter_main)
    return input_grad.reshape(signal.shape), filter_grad


def solution(mesh):
    return jax.shard_map(
        per_device,
        mesh=mesh,
        in_specs=(
            P("dp", "seq", None),
            P("dp", "seq", None),
            P("seq", None),
            P("seq", None),
            P(),
            P(),
        ),
        out_specs=(P("dp", "seq", None), P("seq", None)),
        check_vma=False,
    )
```

```python
import functools
import math

import jax
import jax.numpy as jnp
import numpy as np
from jax import lax
from jax.experimental import pallas as pl
from jax.experimental.pallas import tpu as pltpu
from jax.sharding import PartitionSpec as P

LOGICAL = pl.DeviceIdType.LOGICAL
F32 = jnp.float32
BF16 = jnp.bfloat16
LANES = 128
ROWS = 4
SEQ = 64
DP = 4
ALL = SEQ * DP
HALF = SEQ * ROWS
POINTS = 2 * HALF * LANES
Z, X, Y = 8, 4, 2
VMEM_LIMIT = 58 << 20


def split(values):
    high = values.astype(BF16)
    return high, (values - high.astype(F32)).astype(BF16)


def np_split(values):
    values = values.astype(np.float32)
    high = values.astype(jnp.bfloat16)
    return high, (values - high.astype(np.float32)).astype(jnp.bfloat16)


def tables():
    rows = (ROWS * np.arange(SEQ)[None, :] + np.arange(ROWS)[:, None]).reshape(-1)
    odd = 2 * np.arange(HALF) + 1
    angle = 2 * np.pi / (4 * HALF) * ((odd[:, None] * rows[None, :]) % (4 * HALF))
    first = np.concatenate([np.cos(angle), -np.sin(angle)], axis=0)
    lane = np.arange(LANES)
    angle = 2 * np.pi / (2 * POINTS) * ((odd[:, None] * lane[None, :]) % (2 * POINTS))
    turn = np.concatenate([np.cos(angle), -np.sin(angle)], axis=1).astype(np.float32)
    angle = 2 * np.pi / LANES * ((lane[:, None] * lane[None, :]) % LANES)
    cos, sin = np.cos(angle), np.sin(angle)
    second = np.block([[cos, -sin], [sin, cos]])
    first_high, first_low = np_split(first)
    second_high, second_low = np_split(second)
    return (
        np.concatenate([first_high, first_low], axis=1),
        turn,
        np.concatenate([second_high, second_high, second_low], axis=0),
        np.concatenate([second_high.T, second_high.T, second_low.T], axis=0),
        np.concatenate([first_high.T, first_low.T, first_high.T], axis=1),
    )


def dot(left, right):
    return jnp.dot(left, right, preferred_element_type=F32)


def dot_nt(left, right):
    return lax.dot_general(left, right, (((1,), (1,)), ((), ())), preferred_element_type=F32)


def same(shape, offset=0, factor=1):
    row = lax.broadcasted_iota(jnp.int32, shape, 0)
    column = lax.broadcasted_iota(jnp.int32, shape, 1)
    return jnp.where(column == factor * row + offset, 1.0, 0.0).astype(BF16)


def mix(values, matrix):
    high, low = split(values)
    return dot(jnp.concatenate([high, low, high], axis=1), matrix)


def forward(rows, first, turn, second):
    both = dot(first, jnp.concatenate([rows, rows], axis=0))
    cos, sin = turn[:, :LANES], turn[:, LANES:]
    spectra = []
    for at in range(0, rows.shape[1], LANES):
        real, imag = both[:HALF, at : at + LANES], both[HALF:, at : at + LANES]
        turned = jnp.concatenate([real * cos - imag * sin, real * sin + imag * cos], axis=1)
        spectra.append(mix(turned, second))
    return spectra


def backward(spectra, turn, second_back, first_back):
    cos, sin = turn[:, :LANES], turn[:, LANES:]
    columns = []
    for spectrum in spectra:
        both = mix(spectrum, second_back)
        real, imag = both[:, :LANES], both[:, LANES:]
        columns.append(
            jnp.concatenate([real * cos + imag * sin, imag * cos - real * sin], axis=0)
        )
    high, low = split(jnp.concatenate(columns, axis=1))
    if len(spectra) == 1:
        both = dot(first_back[:, : 2 * HALF], jnp.concatenate([high, low], axis=1))
        rest = dot(first_back[:, 2 * HALF : 4 * HALF], high)
        return both[:, :LANES] + both[:, LANES:] + rest
    return dot(first_back, jnp.concatenate([high, high, low], axis=0))


def conj_product(left, right):
    left_real, left_imag = left[:, :LANES], left[:, LANES:]
    right_real, right_imag = right[:, :LANES], right[:, LANES:]
    return jnp.concatenate(
        [
            left_real * right_real + left_imag * right_imag,
            left_real * right_imag - left_imag * right_real,
        ],
        axis=1,
    )


EARLY = 191
DP_STEPS = ((1, 1), (1, 0), (0, 1), (0, 0))


def hops(near, weight):
    def distance(step):
        up, across, along, side, _ = step
        turns = min(across, X - across) + ((0, 1), (2, 1))[up][side]
        return weight * turns + min(along, Z - along)

    steps = [
        (up, across, along, side, core)
        for along in range(Z)
        for across in range(X)
        for up in range(Y)
        for side, core in near
    ]
    steps.sort(key=lambda step: -distance(step))
    return steps


def spread(wide, values, count):
    for row in range(ROWS):
        wide[pl.ds(0, count), row, :] = values[:, row * LANES : (row + 1) * LANES]
    return wide[pl.ds(0, count)].astype(BF16)


def turn_rows(wide, array):
    for row in range(ROWS):
        wide[:, row, :] = array[pl.ds(row * LANES, LANES), :].astype(F32).T
    return wide[...].astype(BF16)


def gather(wide, start):
    return jnp.concatenate([wide[pl.ds(start, SEQ), row, :] for row in range(ROWS)], axis=0)


def main_kernel(
    signal_hbm, cotangent_hbm, codes_hbm, mask_hbm, exponents, skip, powers_hbm,
    first_hbm, turn_hbm, second_hbm, second_back_hbm, first_back_hbm,
    input_main, filter_main,
    signal, cotangent, codes, mask, powers, first, turn, second, second_back, first_back,
    wide, codes_out, cot_out, sig_out, codes_in, cot_in, sig_in, grad_out, total_out,
    home_grad, home_total,
    cot_spec, send_sem, recv_sem, load_sem,
):
    loads = [
        pltpu.make_async_copy(source, target, load_sem.at[index])
        for index, (source, target) in enumerate(
            (
                (codes_hbm, codes), (cotangent_hbm, cotangent), (signal_hbm, signal),
                (first_hbm, first), (turn_hbm, turn), (second_hbm, second),
                (second_back_hbm, second_back), (first_back_hbm, first_back),
                (powers_hbm, powers), (mask_hbm, mask),
            )
        )
    ]
    for load in loads:
        load.start()
    s, d = lax.axis_index("seq"), lax.axis_index("dp")
    me = s * DP + d
    side, core = d // 2, lax.rem(d, 2)
    q = core * 2 + side
    place = q * SEQ + s
    along = [lax.rem(s + step, Z) for step in range(Z)]
    across = [lax.rem(s // Z + step, X) * Z for step in range(X)]
    up = [lax.rem(s // (Z * X) + step, Y) * (Z * X) for step in range(Y)]
    sides = [lax.rem(side + step, 2) for step in range(2)]
    cores = [lax.rem(core + step, 2) for step in range(2)]

    seq_at = {
        (a, b, c): up[a] + across[b] + along[c]
        for a in range(Y) for b in range(X) for c in range(Z)
    }
    first_at = {step: to_seq * DP for step, to_seq in seq_at.items()}
    dp_at = {
        (a, b): (cores[b] * 2 + sides[a], sides[a] * 2 + cores[b])
        for a in range(2) for b in range(2)
    }
    place_at = {near: to_q * SEQ for near, (to_q, _) in dp_at.items()}

    def target(step):
        seq_step, near = step[:3], step[3:]
        to_seq = seq_at[seq_step]
        return to_seq, place_at[near] + to_seq, first_at[seq_step] + dp_at[near][1]

    everyone = [step for step in hops(DP_STEPS, 1.5) if any(step)]
    barrier = pltpu.get_barrier_semaphore()
    for step in hops(DP_STEPS, 1)[: ALL - 1]:
        pl.semaphore_signal(barrier, inc=1, device_id=target(step)[2], device_id_type=LOGICAL)

    def post(index, source, destination, other):
        pltpu.make_async_remote_copy(
            src_ref=source, dst_ref=destination,
            send_sem=send_sem.at[index], recv_sem=recv_sem.at[index],
            device_id=other, device_id_type=LOGICAL,
        ).start()

    def drain(index, array, count):
        part = array.at[pl.ds(0, count)]
        return pltpu.make_async_remote_copy(
            src_ref=part, dst_ref=part,
            send_sem=send_sem.at[index], recv_sem=recv_sem.at[index],
            device_id=me, device_id_type=LOGICAL,
        )

    loads[0].wait()
    codes_out[...] = spread(wide, dot_nt(same((SEQ, ALL), q * SEQ), codes[...]), SEQ)
    loads[1].wait()
    cot_out[...] = turn_rows(wide, cotangent)
    pl.semaphore_wait(barrier, ALL - 1)

    for step in hops(((0, 0),), 1.5):
        if any(step):
            to_seq, _, other = target(step)
            post(0, codes_out.at[to_seq], codes_in.at[s], other)
    for step in everyone:
        _, to_place, other = target(step)
        post(1, cot_out.at[to_place], cot_in.at[place], other)

    loads[2].wait()
    sig_out[...] = turn_rows(wide, signal)
    for step in everyone:
        _, to_place, other = target(step)
        post(2, sig_out.at[to_place], sig_in.at[place], other)
    codes_in[pl.ds(s, 1)] = codes_out[pl.ds(s, 1)]
    cot_in[pl.ds(place, 1)] = cot_out[pl.ds(place, 1)]
    sig_in[pl.ds(place, 1)] = sig_out[pl.ds(place, 1)]
    for load in loads[3:]:
        load.wait()
    unit = jnp.full((1, LANES), exponents[place].astype(F32), F32)
    scale = jnp.exp2(unit) * (2.0 / POINTS)
    direct = skip[place]

    drain(0, codes_in, SEQ - 1).wait_recv()
    wide[pl.ds(0, SEQ)] = codes_in[...].astype(F32)
    (codes_spec,) = forward(gather(wide, 0).astype(BF16), first[...], turn[...], second[...])

    drain(1, cot_in, ALL - 1).wait_recv()
    wide[...] = cot_in[...].astype(F32)
    cots = [gather(wide, index * SEQ) for index in range(DP)]
    spectra = forward(
        jnp.concatenate(cots, axis=1).astype(BF16), first[...], turn[...], second[...]
    )
    for index, spectrum in enumerate(spectra):
        cot_spec[index] = spectrum
    back = backward(
        [conj_product(codes_spec, spectrum) for spectrum in spectra],
        turn[...], second_back[...], first_back[...],
    )
    for index in range(DP):
        grad = back[:, index * LANES : (index + 1) * LANES] * scale + direct * cots[index]
        part = pl.ds(index * SEQ, SEQ)
        for row in range(ROWS):
            wide[part, row, :] = grad[row * SEQ : (row + 1) * SEQ]
        grad_out[part] = wide[part].astype(BF16)
    for step in everyone[:EARLY]:
        _, to_place, other = target(step)
        post(3, grad_out.at[to_place], home_grad.at[place], other)

    drain(2, sig_in, ALL - 1).wait_recv()
    wide[...] = sig_in[...].astype(F32)
    total_spec = jnp.zeros((HALF, 2 * LANES), F32)
    spectra = forward(
        jnp.concatenate([gather(wide, index * SEQ) for index in range(DP)], axis=1).astype(BF16),
        first[...], turn[...], second[...],
    )
    for index, spectrum in enumerate(spectra):
        total_spec += conj_product(spectrum, cot_spec[index])
    total = backward([total_spec], turn[...], second_back[...], first_back[...])
    total = total * (2.0 / POINTS)
    for row in range(ROWS):
        wide[pl.ds(0, SEQ), row, :] = total[row * SEQ : (row + 1) * SEQ]
    total_out[...] = wide[pl.ds(0, SEQ)].astype(BF16)
    for step in hops(((0, 0), (1, 0)), 1.5):
        if any(step):
            to_seq, _, other = target(step)
            post(4, total_out.at[to_seq], home_total.at[s + side * SEQ], other)
    for step in everyone[EARLY:]:
        _, to_place, other = target(step)
        post(3, grad_out.at[to_place], home_grad.at[place], other)
    home_total[pl.ds(s + side * SEQ, 1)] = total_out[pl.ds(s, 1)]
    home_grad[pl.ds(place, 1)] = grad_out[pl.ds(place, 1)]

    half = 2 * SEQ
    channels = pl.ds(pl.multiple_of(core * half, LANES), half)
    factor = jnp.exp2(powers[...].astype(F32))
    factor = jnp.where(core == 0, factor[:, :half], factor[:, half:])
    drain(4, home_total, half - 1).wait_recv()
    wide[pl.ds(0, half)] = home_total[...].astype(F32)
    for row in range(ROWS):
        part = pl.ds(row * LANES, LANES)
        value = wide[pl.ds(0, half), row, :].T
        value = mask[part, channels].astype(F32) * factor * value
        filter_main[core, part, :] = value.astype(BF16)
    across_core = pltpu.make_async_remote_copy(
        src_ref=filter_main.at[core], dst_ref=filter_main.at[core],
        send_sem=send_sem.at[5], recv_sem=recv_sem.at[5],
        device_id=me + 1 - 2 * core, device_id_type=LOGICAL,
    )
    across_core.start()
    drain(3, home_grad, ALL - 1).wait_recv()
    wide[...] = home_grad[...].astype(F32)
    for row in range(ROWS):
        input_main[pl.ds(row * LANES, LANES), :] = wide[:, row, :].T.astype(BF16)
    drain(0, codes_out, SEQ - 1).wait_send()
    drain(1, cot_out, ALL - 1).wait_send()
    drain(2, sig_out, ALL - 1).wait_send()
    drain(3, grad_out, ALL - 1).wait_send()
    drain(4, home_total, half - 1).wait_send()
    across_core.wait()


def last_kernel(input_main, filter_main, input_grad, filter_grad, held, sem):
    stores = [pltpu.make_async_copy(input_main, input_grad, sem.at[ROWS])]
    stores[0].start()
    for row in range(ROWS):
        part = pl.ds(row * LANES, LANES)
        for index in range(2):
            value = filter_main[index, part, :].astype(F32) * (1.0 / math.sqrt(DP * HALF * LANES))
            held[part, pl.ds(index * LANES, LANES)] = value
        stores.append(pltpu.make_async_copy(held.at[part], filter_grad.at[part], sem.at[row]))
        stores[-1].start()
    for store in stores:
        store.wait()


def per_device(signal, cotangent, filter_codes, keep_mask, exponents, skip):
    span, width = signal.shape[1], signal.shape[2]
    smem = pl.BlockSpec(memory_space=pltpu.SMEM)
    hbm = pl.BlockSpec(memory_space=pltpu.HBM)
    vmem = pl.BlockSpec(memory_space=pltpu.VMEM)
    constants = [jnp.asarray(table) for table in tables()]
    message = (ROWS, LANES)
    results = (
        jax.ShapeDtypeStruct((span, width), BF16),
        jax.ShapeDtypeStruct((span, width), F32),
    )
    input_main, filter_main = pl.pallas_call(
        main_kernel,
        out_shape=(pltpu.VMEM((span, width), BF16), pltpu.VMEM((2, span, width // 2), BF16)),
        in_specs=[hbm] * 4 + [smem] * 2 + [hbm] * 6,
        out_specs=(vmem, vmem),
        scratch_shapes=[
            pltpu.VMEM((span, width), BF16),
            pltpu.VMEM((span, width), BF16),
            pltpu.VMEM((span, width), BF16),
            pltpu.VMEM((span, width), jnp.int32),
            pltpu.VMEM((1, width), jnp.int32),
            *[pltpu.VMEM(table.shape, table.dtype) for table in constants],
            pltpu.VMEM((ALL,) + message, F32),
            pltpu.VMEM((SEQ,) + message, BF16),
            pltpu.VMEM((ALL,) + message, BF16),
            pltpu.VMEM((ALL,) + message, BF16),
            pltpu.VMEM((SEQ,) + message, BF16),
            pltpu.VMEM((ALL,) + message, BF16),
            pltpu.VMEM((ALL,) + message, BF16),
            pltpu.VMEM((ALL,) + message, BF16),
            pltpu.VMEM((SEQ,) + message, BF16),
            pltpu.VMEM((ALL,) + message, BF16),
            pltpu.VMEM((2 * SEQ,) + message, BF16),
            pltpu.VMEM((DP, HALF, 2 * LANES), F32),
            pltpu.SemaphoreType.DMA((6,)),
            pltpu.SemaphoreType.DMA((6,)),
            pltpu.SemaphoreType.DMA((10,)),
        ],
        compiler_params=pltpu.CompilerParams(
            collective_id=0, has_side_effects=True, vmem_limit_bytes=VMEM_LIMIT
        ),
        name="main",
    )(
        signal.reshape(span, width), cotangent.reshape(span, width), filter_codes, keep_mask,
        exponents, skip, exponents.reshape(1, width), *constants,
    )
    input_grad, filter_grad = pl.pallas_call(
        last_kernel,
        out_shape=results,
        in_specs=[vmem, vmem],
        out_specs=(hbm, hbm),
        scratch_shapes=[
            pltpu.VMEM((span, width), F32),
            pltpu.SemaphoreType.DMA((ROWS + 1,)),
        ],
        compiler_params=pltpu.CompilerParams(vmem_limit_bytes=4 << 20),
        name="last",
    )(input_main, filter_main)
    return input_grad.reshape(signal.shape), filter_grad


def solution(mesh):
    return jax.shard_map(
        per_device,
        mesh=mesh,
        in_specs=(
            P("dp", "seq", None),
            P("dp", "seq", None),
            P("seq", None),
            P("seq", None),
            P(),
            P(),
        ),
        out_specs=(P("dp", "seq", None), P("seq", None)),
        check_vma=False,
    )
```
